32 devices in a mesh: rows: 16 (over z, y, x), rep: 2 (over core).
Axes of the slice: x: 2, y: 2, z: 4, core: 2. Of those that a mesh axis runs over, the one named last changes fastest.
Arguments:
- margin_blocks: float32 [64, 16, 128, 128], P('rows', 'rep'), may hold values from -1 to 1
- margin_cols: int32 [64, 16], P('rows', 'rep'), may hold values from 0 to 63, as said below
- factor_blocks: float32 [64, 16, 128, 128], P('rows'), may hold values from -0.5 to 0.5
- factor_cols: int32 [64, 16], P('rows'), may hold values from 0 to 63, as said below
- product_cols: int32 [64, 24], P('rows'), may hold values from 0 to 63, as said below
- metric_cols: int32 [64, 24], P('rows'), may hold values from 0 to 63, as said below
Outputs:
- product: float32 [64, 24, 128, 128], P('rows', 'rep')
- metric: float32 [64, 24, 128, 128], P('rows', 'rep')
The draws below stay inside these ranges and needn't reach their ends.
Inputs may be any that keep to these rules, and one draw needn't show every extreme that they name: `margin_cols`: each block row holds 16 distinct block columns, its own index among them, each within 8 of the row index cyclically modulo 64. `factor_cols`: each block row holds 16 distinct block columns, each in the block rows of an index of rows at most 2 away from the row's own (column // 4 against row // 4, cyclically); every block column is named by exactly 16 block rows. `product_cols`: each block row holds 24 distinct block columns, its own index among them, each within 16 of the row index cyclically. `metric_cols`: each block row holds 24 distinct block columns, its own index among them, each within 16 of the row index cyclically.
All inputs are finite; a program needn't handle non-finite values.
Results may differ from the reference program's by a relative error of at most 0.0003.
Values sent between devices are 32-bit elements; how exact they have to be, the bound alone decides.
A program may use at most 192 MiB of HBM per device.

```python
import jax
import jax.numpy as jnp
from jax import lax

BLOCK = 128
ROWS_DEV = 4
SLOTS_S = 16
SLOTS_Z = 16
SLOTS_Y = 24
SLOTS_X = 24
BLOCKS = 64


def band_pattern(key, count, reach):
    span = 2 * reach + 1
    scores = jax.random.randint(key, (BLOCKS, span), 0, 1 << 20) * span + jnp.arange(span, dtype=jnp.int32)[None, :]
    scores = scores.at[:, reach].set(jnp.int32(1 << 30))
    chosen_values, chosen_offsets = lax.top_k(scores, count)
    row_index = jnp.arange(BLOCKS, dtype=jnp.int32)[:, None]
    return ((row_index + chosen_offsets.astype(jnp.int32) - reach) % BLOCKS).astype(jnp.int32)


def draw_margin_cols(key, part):
    return band_pattern(jax.random.fold_in(key, 11), SLOTS_S, 2 * ROWS_DEV)


def draw_product_cols(key, part):
    return band_pattern(jax.random.fold_in(key, 12), SLOTS_Y, 4 * ROWS_DEV)


def draw_metric_cols(key, part):
    return band_pattern(jax.random.fold_in(key, 13), SLOTS_X, 4 * ROWS_DEV)


def random_orders(key, groups):
    scores = jax.random.randint(key, (groups, 5, ROWS_DEV), 0, 1 << 20) * ROWS_DEV + jnp.arange(ROWS_DEV, dtype=jnp.int32)
    return jnp.argsort(scores, axis=-1, stable=True).astype(jnp.int32)


def draw_factor_cols(key, part):
    groups = BLOCKS // ROWS_DEV
    key = jax.random.fold_in(key, 14)
    key_counts, key_subset, key_place, key_shift = jax.random.split(key, 4)
    even_counts = SLOTS_Z // 5 + (jnp.arange(5) < SLOTS_Z % 5).astype(jnp.int32)
    counts = even_counts[jax.random.permutation(key_counts, 5)]
    bounds = jnp.cumsum(counts)
    starts = bounds - counts
    slot_index = jnp.arange(SLOTS_Z, dtype=jnp.int32)
    band_index = jnp.sum((slot_index[:, None] >= bounds[None, :]).astype(jnp.int32), axis=1)
    within = slot_index - starts[band_index]
    subset_order = random_orders(key_subset, groups)
    place_order = random_orders(key_place, groups)
    shift_order = random_orders(key_shift, groups)
    row_index = jnp.arange(BLOCKS, dtype=jnp.int32)
    group_index = (row_index // ROWS_DEV)[:, None]
    inner_index = (row_index % ROWS_DEV)[:, None]
    chosen_shift = subset_order[group_index, band_index[None, :], within[None, :]]
    start_shift = shift_order[group_index, band_index[None, :], inner_index]
    target_place = place_order[group_index, band_index[None, :], (start_shift + chosen_shift) % ROWS_DEV]
    target_group = (group_index + band_index[None, :] - 2) % groups
    return (target_group * ROWS_DEV + target_place).astype(jnp.int32)


def shard_levels(key, shape, shards, smallest, top_value):
    def one(dim, blocks):
        draws = jax.random.uniform(jax.random.fold_in(jax.random.fold_in(key, 6), dim), (blocks,), jnp.float32, smallest / len(shards), top_value / len(shards))
        return jnp.repeat(jnp.exp(draws), shape[dim] // blocks).reshape((-1,) + (1,) * (len(shape) - dim - 1))

    gain = one(*shards[0])
    for cut in shards[1:]:
        gain = gain * one(*cut)
    return gain


def noise(rng, shape, scale, bound, pieces=(), kind=jnp.bfloat16):
    array = scale * jax.random.normal(rng, shape, jnp.float32)
    if pieces:
        array = array * shard_levels(rng, shape, pieces, -0.22, 0.18)
    return jnp.clip(array, -bound, bound).astype(kind)


def setup_inputs(seed: int = 0) -> dict:
    splits = jax.random.split(jax.random.key(seed), 7)
    margin_blocks = noise(splits[0], (BLOCKS, SLOTS_S, BLOCK, BLOCK), (BLOCK // 4) ** -0.5, 1.0, ((0, 16), (1, 2)), jnp.float32)
    margin_cols = draw_margin_cols(jax.random.fold_in(splits[6], 71), 0)
    factor_blocks = noise(splits[2], (BLOCKS, SLOTS_Z, BLOCK, BLOCK), BLOCK ** -0.5, 0.5, ((0, 16),), jnp.float32)
    factor_cols = draw_factor_cols(jax.random.fold_in(splits[6], 71), 0)
    product_cols = draw_product_cols(jax.random.fold_in(splits[6], 71), 0)
    metric_cols = draw_metric_cols(jax.random.fold_in(splits[6], 71), 0)
    return dict(margin_blocks=margin_blocks, margin_cols=margin_cols, factor_blocks=factor_blocks, factor_cols=factor_cols, product_cols=product_cols, metric_cols=metric_cols)


HIGHEST = lax.Precision.HIGHEST


def reference(margin_blocks, margin_cols, factor_blocks, factor_cols, product_cols, metric_cols):
    def product_row(packed):
        margin_row, column_row, kept_row = packed
        picked = factor_blocks[column_row]
        partial_terms = jnp.einsum('kab,kmbc->kmac', margin_row, picked, precision=HIGHEST)
        selector = (factor_cols[column_row][:, :, None] == kept_row[None, None, :]).astype(jnp.float32)
        return jnp.einsum('kmy,kmac->yac', selector, partial_terms, precision=HIGHEST)

    product = lax.map(product_row, (margin_blocks, margin_cols, product_cols))
    flat_cols = factor_cols.reshape(-1)
    flat_blocks = factor_blocks.reshape(-1, BLOCK, BLOCK)

    def metric_row(packed):
        target, kept_row = packed
        positions = jnp.nonzero(flat_cols == target, size=SLOTS_Z)[0].astype(jnp.int32)
        source_rows = (positions // SLOTS_Z).astype(jnp.int32)
        factor_here = flat_blocks[positions]
        product_here = product[source_rows]
        partial_terms = jnp.einsum('tba,tybc->tyac', factor_here, product_here, precision=HIGHEST)
        selector = (product_cols[source_rows][:, :, None] == kept_row[None, None, :]).astype(jnp.float32)
        return jnp.einsum('tyx,tyac->xac', selector, partial_terms, precision=HIGHEST)

    metric = lax.map(metric_row, (jnp.arange(BLOCKS, dtype=jnp.int32), metric_cols))
    return product, metric
```

```python
import jax
import jax.numpy as jnp
from jax import lax
from jax.experimental import pallas as pl
from jax.experimental.pallas import tpu as pltpu
from jax.sharding import PartitionSpec as P

GROUP = 4
CODE = 1024


def flip_x(s, n):
    return s ^ 1


def flip_y(s, n):
    return s ^ 2


def step_z(s, n):
    return (s + 4) % n if s % 4 < 2 else (s - 4) % n


def hop(array, target, among=(0, 1, 2, 3)):
    n = lax.axis_size("rows")
    return lax.ppermute(array, "rows", [(s, target(s, n)) for s in range(n) if s % 4 in among])


def swap(array):
    return lax.ppermute(array, "rep", [(0, 1), (1, 0)])


def halo(chunks, inner):
    over_x = [hop(c, flip_x) for c in chunks]
    over_y = [hop(c, flip_y) for c in chunks]
    over_z = [hop(c, step_z) for c in over_y]
    second = []
    for y, z in zip(over_y, over_z):
        early = hop(y, flip_x, (0, 3))
        late = hop(z, flip_x, (1, 2))
        second.append(jnp.where(inner, early, late))
    return [over_x, over_y, over_z, second]


def block_products(table, groups, sources, moves, lhs_parts, pool_blocks, transposed, outs):
    rows, block = lhs_parts[0].shape[0], lhs_parts[0].shape[2]
    slots = sum(part.shape[1] for part in lhs_parts)
    source_count, part_count = len(sources), len(lhs_parts)

    def kernel(*refs):
        groups_ref, table_ref = refs[:2]
        source_refs = refs[2 : 2 + source_count]
        lhs_refs = refs[2 + source_count : 2 + source_count + part_count]
        out_ref, pool, high, low, sems = refs[2 + source_count + part_count :]
        copies = []
        for index, (source, at, dst, count) in enumerate(moves):
            copy = pltpu.make_async_copy(
                source_refs[source].at[at], pool.at[pl.ds(dst, count)], sems.at[index]
            )
            copy.start()
            copies.append(copy)
        pool[pool_blocks] = jnp.zeros((block, block), jnp.float32)

        def split_row(row, carry):
            base = row * slots
            for ref in lhs_refs:
                for s in range(ref.shape[1]):
                    value = ref[row, s]
                    if transposed:
                        value = value.T
                    top = value.astype(jnp.bfloat16)
                    high[base + s] = top
                    low[base + s] = (value - top.astype(jnp.float32)).astype(jnp.bfloat16)
                base = base + ref.shape[1]
            return carry

        lax.fori_loop(0, rows, split_row, 0)
        for copy in copies:
            copy.wait()

        def one_output(o, carry):
            row = o // outs

            def one_group(g, total):
                left, right = [], []
                for e in range(GROUP):
                    code = table_ref[o * slots + g * GROUP + e]
                    s = row * slots + code // CODE
                    value = pool[code % CODE]
                    top = value.astype(jnp.bfloat16)
                    rest = (value - top.astype(jnp.float32)).astype(jnp.bfloat16)
                    left += [high[s], high[s], low[s]]
                    right += [top, rest, top]
                return total + jnp.dot(
                    jnp.concatenate(left, axis=1),
                    jnp.concatenate(right, axis=0),
                    preferred_element_type=jnp.float32,
                )

            out_ref[o] = lax.fori_loop(
                0, groups_ref[o], one_group, jnp.zeros((block, block), jnp.float32)
            )
            return carry

        lax.fori_loop(0, rows * outs, one_output, 0)

    in_specs = (
        [pl.BlockSpec(memory_space=pltpu.SMEM)] * 2
        + [pl.BlockSpec(memory_space=pl.ANY)] * source_count
        + [pl.BlockSpec(memory_space=pltpu.VMEM)] * part_count
    )
    result = pl.pallas_call(
        kernel,
        out_shape=jax.ShapeDtypeStruct((rows * outs, block, block), jnp.float32),
        in_specs=in_specs,
        out_specs=pl.BlockSpec(memory_space=pltpu.VMEM),
        scratch_shapes=[
            pltpu.VMEM((pool_blocks + 1, block, block), jnp.float32),
            pltpu.VMEM((rows * slots, block, block), jnp.bfloat16),
            pltpu.VMEM((rows * slots, block, block), jnp.bfloat16),
            pltpu.SemaphoreType.DMA((len(moves),)),
        ],
        compiler_params=pltpu.CompilerParams(vmem_limit_bytes=52 * 1024 * 1024),
        cost_estimate=pl.CostEstimate(
            flops=rows * outs * 10 * 6 * block**3 * 4,
            bytes_accessed=(pool_blocks + rows * (slots + outs)) * block * block * 4,
            transcendentals=0,
        ),
    )(groups.reshape(-1), table.reshape(-1), *sources, *lhs_parts)
    return result.reshape(rows, outs, block, block)


def packed_list(found, codes, dummy):
    slots = found.shape[-1]
    index = jnp.arange(slots, dtype=jnp.int32)
    before = (index[:, None] > index[None, :]).astype(jnp.int32)
    rank = jnp.sum(found[..., None, :] * before, axis=-1)
    count = jnp.sum(found, axis=-1)
    chosen = found[..., None, :] * (rank[..., None, :] == index[:, None]).astype(jnp.int32)
    listed = jnp.sum(chosen * codes[..., None, :], axis=-1)
    listed = jnp.where(index < count[..., None], listed, dummy)
    return listed, (count + GROUP - 1) // GROUP


def shards(margin_blocks, margin_cols, factor_blocks, factor_cols, product_cols, metric_cols):
    rows, slots, block = factor_blocks.shape[:3]
    kept, kept_x = product_cols.shape[1], metric_cols.shape[1]
    half_rows, half_kept, half_x = rows // 2, kept // 2, kept_x // 2
    n = lax.axis_size("rows")
    r = lax.axis_index("rows")
    q = lax.axis_index("rep")
    place = r % 4
    inner = (place == 1) | (place == 2)
    int32 = jnp.int32

    mine = lax.dynamic_slice_in_dim(factor_blocks, q * half_rows, half_rows, 0)
    near = halo([mine[c] for c in range(half_rows)], inner)
    their_margin = swap(margin_blocks)
    near_theirs = [[swap(c) for c in chunks] for chunks in near]

    sign_x = 1 - 2 * (place % 2)
    sign_y = 2 - 4 * (place // 2)
    patterns = jnp.concatenate([factor_cols, product_cols], axis=1)
    by_offset = [
        lax.ppermute(patterns, "rows", [(s, (s - o) % n) for s in range(n)]) if o else patterns
        for o in (-2, -1, 0, 1, 2)
    ]
    offsets = jnp.stack([0 * sign_x, sign_x, sign_y, -sign_y, -sign_x]).astype(int32)
    which = (offsets[:, None] == jnp.arange(-2, 3, dtype=int32)[None, :]).astype(int32)
    near_patterns = jnp.sum(which[:, :, None, None] * jnp.stack(by_offset)[None], axis=1)
    near_patterns = near_patterns.reshape(5 * rows, slots + kept)
    near_factor_cols = near_patterns[:, :slots]
    near_product_cols = near_patterns[:, slots:]
    near_index = jnp.arange(5 * rows, dtype=int32)
    row_of, slot_of = near_index % rows, near_index // rows
    swapped = slot_of * rows + ((row_of // half_rows) ^ q) * half_rows + row_of % half_rows
    factor_at = jnp.where(slot_of == 0, near_index, swapped).astype(int32)

    columns = jnp.concatenate([margin_cols, swap(margin_cols)], axis=1)
    offset = (columns // rows - r + 2) % n - 2
    slot = jnp.sum((offset[..., None] == offsets) * jnp.arange(5, dtype=int32), axis=-1)
    picked = (slot * rows + columns % rows)[..., None] == near_index
    picked = picked.astype(int32)
    picked_cols = jnp.sum(picked[..., None] * near_factor_cols, axis=2)
    picked_at = jnp.sum(picked * factor_at, axis=2)
    my_product_cols = lax.dynamic_slice_in_dim(product_cols, q * half_kept, half_kept, 1)
    match = (picked_cols[:, None] == my_product_cols[:, :, None, None]).astype(int32)
    m_index = jnp.arange(slots, dtype=int32)
    k_index = jnp.arange(columns.shape[1], dtype=int32)
    code = k_index[:, None] * CODE + picked_at[:, None, :, None] * slots + m_index
    table, groups = packed_list(
        jnp.sum(match, axis=-1), jnp.sum(match * code, axis=-1), 5 * rows * slots
    )

    sources, moves = [factor_blocks], []
    for row in range(rows):
        moves.append((0, row, row * slots, slots))
    for j in range(4):
        for h, chunks in enumerate((near[j], near_theirs[j])):
            for c, chunk in enumerate(chunks):
                dst = ((j + 1) * rows + h * half_rows + c) * slots
                moves.append((len(sources), slice(None), dst, slots))
                sources.append(chunk)
    product = block_products(
        table,
        groups,
        sources,
        moves,
        [margin_blocks, their_margin],
        5 * rows * slots,
        False,
        half_kept,
    )

    chunks = [product[:half_rows], product[half_rows:]]
    near_product = [chunks] + halo(chunks, inner)
    near_product_theirs = [[swap(c) for c in part] for part in near_product]

    targets = r * rows + jnp.arange(rows, dtype=int32)
    hit = (near_factor_cols[None] == targets[:, None, None]).astype(int32)
    held = jnp.sum(hit, axis=-1)
    at = jnp.sum(hit * (factor_at[:, None] * slots + m_index), axis=-1)
    entry_code, _ = packed_list(held, near_index * (5 * rows * slots) + at, 0)
    entry_code = entry_code[:, :slots]
    entry_row = entry_code // (5 * rows * slots)
    entry_at = entry_code % (5 * rows * slots)
    flat = jnp.concatenate(
        [factor_blocks.reshape(-1, block, block)]
        + [c for j in range(4) for part in (near[j], near_theirs[j]) for c in part]
    )
    entries = flat[entry_at]
    order = jnp.where(q == 0, near_product_cols, jnp.roll(near_product_cols, half_kept, axis=1))
    entry_pick = (entry_row[..., None] == near_index).astype(int32)
    entry_cols = jnp.sum(entry_pick[..., None] * order, axis=2)
    my_metric_cols = lax.dynamic_slice_in_dim(metric_cols, q * half_x, half_x, 1)
    match = (entry_cols[:, None] == my_metric_cols[:, :, None, None]).astype(int32)
    y_index = jnp.arange(kept, dtype=int32)
    code = m_index[:, None] * CODE + entry_row[:, None, :, None] * kept + y_index
    table, groups = packed_list(
        jnp.sum(match, axis=-1), jnp.sum(match * code, axis=-1), 5 * rows * kept
    )

    sources, moves = [], []
    for j in range(5):
        for h, parts in enumerate((near_product[j], near_product_theirs[j])):
            for c, chunk in enumerate(parts):
                for row in range(half_rows):
                    dst = (j * rows + c * half_rows + row) * kept + h * half_kept
                    moves.append((len(sources), row, dst, half_kept))
                sources.append(chunk)
    metric = block_products(
        table, groups, sources, moves, [entries], 5 * rows * kept, True, half_x
    )
    return (product, metric)


def solution(mesh):
    return jax.shard_map(
        shards,
        mesh=mesh,
        in_specs=(
            P("rows", "rep", None, None),
            P("rows", "rep"),
            P("rows", None, None, None),
            P("rows", None),
            P("rows", None),
            P("rows", None),
        ),
        out_specs=(P("rows", "rep", None, None), P("rows", "rep", None, None)),
        check_vma=False,
    )
```

```python
import jax
import jax.numpy as jnp
from jax import lax
from jax.experimental import pallas as pl
from jax.experimental.pallas import tpu as pltpu
from jax.sharding import PartitionSpec as P

MESH = pl.DeviceIdType.MESH
CHUNKS = 8
GROUP = 4
TOGETHER = 2
CODE = 1024


def swap(array):
    return lax.ppermute(array, "rep", [(0, 1), (1, 0)])


def fetch_halo(sent, sent_base, swapped, chunks, size, collective_id):
    block = sent.shape[-1]
    at_x, at_y, at_z, at_second, at_swap, at_way = 0, 1, 2, 3, 8, 9

    def kernel(sent_ref, swapped_ref, out_ref, send_sem, recv_sem):
        n = lax.axis_size("rows")
        r = lax.axis_index("rows")
        q = lax.axis_index("rep")
        px, py = r % 2, (r // 2) % 2
        to_x = r + 1 - 2 * px
        to_y = r + 2 - 4 * py
        to_z = (r + n + 4 - 8 * py) % n
        from_z = (r + n - 4 + 8 * py) % n
        outer = px == py
        barrier = pltpu.get_barrier_semaphore()
        for rows, rep in ((to_x, q), (to_y, q), (from_z, q), (r, 1 - q)):
            pl.semaphore_signal(barrier, inc=1, device_id=(rows, rep), device_id_type=MESH)
        pl.semaphore_wait(barrier, 4)

        def span(c):
            return pl.ds(c * size, size)

        def copy(src, kind, place, c, target):
            return pltpu.make_async_remote_copy(
                src_ref=src,
                dst_ref=out_ref.at[place, span(c)],
                send_sem=send_sem.at[kind, c],
                recv_sem=recv_sem.at[place, c],
                device_id=target,
                device_id_type=MESH,
            )

        def own(c):
            return sent_ref.at[pl.ds(sent_base(q) + c * size, size)]

        def over_x(c):
            return copy(own(c), 0, at_x, c, (to_x, q))

        def over_y(c):
            return copy(own(c), 1, at_y, c, (to_y, q))

        def over_z(c):
            return copy(out_ref.at[at_y, span(c)], 2, at_z, c, (to_z, q))

        def second_x(c, held):
            return copy(out_ref.at[held, span(c)], 3, at_second, c, (to_x, q))

        def second_y(c):
            place = jnp.where(outer, at_second, at_way)
            return copy(out_ref.at[at_x, span(c)], 3, place, c, (to_y, q))

        def second_z(c):
            return copy(out_ref.at[at_way, span(c)], 9, at_second, c, (to_z, q))

        def share(place, c):
            return copy(out_ref.at[place, span(c)], 4 + place, 4 + place, c, (r, 1 - q))

        def own_share(c):
            return copy(swapped_ref.at[span(c)], 8, at_swap, c, (r, 1 - q))

        def arrived(place, c):
            copy(out_ref.at[place, span(c)], 0, place, c, (r, 1 - q)).wait_recv()

        pairs = [(c, c + 1) for c in range(0, chunks, 2)]
        x_order = [b for a, b in pairs] + [a for a, b in pairs]
        y_order = [a for a, b in pairs] + [b for a, b in pairs]
        ahead = 2
        for i in range(ahead):
            over_x(x_order[i]).start()
            over_y(y_order[i]).start()
        for i in range(chunks):
            c = x_order[i]
            arrived(at_x, c)
            if c % 2:
                second_y(c).start()
            if i + ahead < chunks:
                over_x(x_order[i + ahead]).start()
            share(at_x, c).start()
            own_share(i).start()
            c = y_order[i]
            arrived(at_y, c)
            over_z(c).start()
            if c % 2 == 0:

                @pl.when(outer)
                def _(c=c):
                    second_x(c, at_y).start()

            if i + ahead < chunks:
                over_y(y_order[i + ahead]).start()
            share(at_y, c).start()
            if i >= 1:
                c = y_order[i - 1]
                arrived(at_z, c)
                if c % 2 == 0:

                    @pl.when(jnp.logical_not(outer))
                    def _(c=c):
                        second_x(c, at_z).start()

                share(at_z, c).start()
            if 1 <= i <= len(pairs):
                c = x_order[i - 1]

                @pl.when(outer)
                def _(c=c):
                    arrived(at_way, c)
                    second_z(c).start()

            if i >= len(pairs):
                for c in pairs[i - len(pairs)]:
                    arrived(at_second, c)
                    share(at_second, c).start()
        c = y_order[-1]
        arrived(at_z, c)
        share(at_z, c).start()
        for c in range(chunks):
            for place in (4, 5, 6, 7, at_swap):
                arrived(place, c)
        for c in range(chunks):
            over_x(c).wait_send()
            over_y(c).wait_send()
            over_z(c).wait_send()
            second_x(c, at_z).wait_send()
            if c % 2:

                @pl.when(outer)
                def _(c=c):
                    second_z(c).wait_send()

            for place in (at_x, at_y, at_z, at_second):
                share(place, c).wait_send()
            own_share(c).wait_send()

    return pl.pallas_call(
        kernel,
        out_shape=jax.ShapeDtypeStruct((10, chunks * size, block, block), jnp.float32),
        in_specs=[pl.BlockSpec(memory_space=pl.ANY)] * 2,
        out_specs=pl.BlockSpec(memory_space=pl.ANY),
        scratch_shapes=[
            pltpu.SemaphoreType.DMA((10, chunks)),
            pltpu.SemaphoreType.DMA((10, chunks)),
        ],
        compiler_params=pltpu.CompilerParams(collective_id=collective_id, has_side_effects=True),
    )(sent, swapped)


def block_products(table, groups, sources, moves, lhs_moves, rows, slots, pool_blocks, entries, outs):
    block = sources[0].shape[-1]
    source_count = len(sources)
    transposed = entries is not None
    scalars = [groups, table] + ([entries] if transposed else [])
    scalar_count = len(scalars)

    def kernel(*refs):
        groups_ref, table_ref = refs[:2]
        source_refs = refs[scalar_count : scalar_count + source_count]
        out_ref, pool, lhs, high, low, sems, lhs_sems = refs[scalar_count + source_count :]

        def moved(index, move, target, semaphores):
            source, at, dst, count = move
            return pltpu.make_async_copy(
                source_refs[source].at[at], target.at[pl.ds(dst, count)], semaphores.at[index]
            )

        lhs_copies = [moved(i, move, lhs, lhs_sems) for i, move in enumerate(lhs_moves)]
        copies = [moved(i, move, pool, sems) for i, move in enumerate(moves)]
        for copy in lhs_copies:
            copy.start()
        if transposed:
            first, second = source_refs[-2:]
            bound = first.shape[0]

            def fetch(i, carry):
                code = refs[2][i]

                @pl.when(code < bound)
                def _():
                    pltpu.make_async_copy(first.at[code], lhs.at[i], lhs_sems.at[i]).start()

                @pl.when(code >= bound)
                def _():
                    pltpu.make_async_copy(
                        second.at[code - bound], lhs.at[i], lhs_sems.at[i]
                    ).start()

                return carry

            lax.fori_loop(0, rows * slots, fetch, 0)
        for copy in copies:
            copy.start()
        pool[pool_blocks] = jnp.zeros((block, block), jnp.float32)
        for copy in lhs_copies:
            copy.wait()

        def split(index, carry):
            for e in range(4):
                i = index * 4 + e
                if transposed:
                    pltpu.make_async_copy(source_refs[-2].at[0], lhs.at[i], lhs_sems.at[i]).wait()
                value = lhs[i].T if transposed else lhs[i]
                top = value.astype(jnp.bfloat16)
                high[i] = top
                low[i] = (value - top.astype(jnp.float32)).astype(jnp.bfloat16)
            return carry

        lax.fori_loop(0, rows * slots // 4, split, 0)
        for copy in copies:
            copy.wait()

        def term(o, g):
            row = o // outs
            left, right = [], []
            for e in range(GROUP):
                code = table_ref[o * slots + g * GROUP + e]
                s = row * slots + code // CODE
                value = pool[code % CODE]
                top = value.astype(jnp.bfloat16)
                rest = (value - top.astype(jnp.float32)).astype(jnp.bfloat16)
                left += [high[s], high[s], low[s]]
                right += [top, rest, top]
            return jnp.dot(
                jnp.concatenate(left, axis=1),
                jnp.concatenate(right, axis=0),
                preferred_element_type=jnp.float32,
            )

        def some_outputs(index, carry):
            first = index * TOGETHER
            steps = groups_ref[first]
            for e in range(1, TOGETHER):
                steps = jnp.maximum(steps, groups_ref[first + e])

            def one_group(g, totals):
                return tuple(totals[e] + term(first + e, g) for e in range(TOGETHER))

            zero = jnp.zeros((block, block), jnp.float32)
            totals = lax.fori_loop(0, steps, one_group, (zero,) * TOGETHER)
            for e in range(TOGETHER):
                out_ref[first + e] = totals[e]
            return carry

        lax.fori_loop(0, rows * outs // TOGETHER, some_outputs, 0)

    in_specs = (
        [pl.BlockSpec(memory_space=pltpu.SMEM)] * scalar_count
        + [pl.BlockSpec(memory_space=pl.ANY)] * source_count
    )
    result = pl.pallas_call(
        kernel,
        out_shape=jax.ShapeDtypeStruct((rows * outs, block, block), jnp.float32),
        in_specs=in_specs,
        out_specs=pl.BlockSpec(memory_space=pltpu.VMEM),
        scratch_shapes=[
            pltpu.VMEM((pool_blocks + 1, block, block), jnp.float32),
            pltpu.VMEM((rows * slots, block, block), jnp.float32),
            pltpu.VMEM((rows * slots, block, block), jnp.bfloat16),
            pltpu.VMEM((rows * slots, block, block), jnp.bfloat16),
            pltpu.SemaphoreType.DMA((len(moves),)),
            pltpu.SemaphoreType.DMA((rows * slots,)),
        ],
        compiler_params=pltpu.CompilerParams(vmem_limit_bytes=52 * 1024 * 1024),
        cost_estimate=pl.CostEstimate(
            flops=rows * outs * 10 * 6 * block**3 * 4,
            bytes_accessed=(pool_blocks + rows * (slots + outs)) * block * block * 4,
            transcendentals=0,
        ),
    )(*[scalar.reshape(-1) for scalar in scalars], *sources)
    return result.reshape(rows, outs, block, block)


def packed_list(found, codes, dummy):
    slots = found.shape[-1]
    index = jnp.arange(slots, dtype=jnp.int32)
    before = (index[:, None] > index[None, :]).astype(jnp.int32)
    rank = jnp.sum(found[..., None, :] * before, axis=-1)
    count = jnp.sum(found, axis=-1)
    chosen = found[..., None, :] * (rank[..., None, :] == index[:, None]).astype(jnp.int32)
    listed = jnp.sum(chosen * codes[..., None, :], axis=-1)
    listed = jnp.where(index < count[..., None], listed, dummy)
    return listed, (count + GROUP - 1) // GROUP


def shards(margin_blocks, margin_cols, factor_blocks, factor_cols, product_cols, metric_cols):
    rows, slots, block = factor_blocks.shape[:3]
    kept, kept_x = product_cols.shape[1], metric_cols.shape[1]
    half_rows, half_kept, half_x = rows // 2, kept // 2, kept_x // 2
    n = lax.axis_size("rows")
    r = lax.axis_index("rows")
    q = lax.axis_index("rep")
    place = r % 4
    int32 = jnp.int32

    sign_x = 1 - 2 * (place % 2)
    sign_y = 2 - 4 * (place // 2)
    patterns = jnp.concatenate([factor_cols, product_cols], axis=1)
    by_offset = [
        lax.ppermute(patterns, "rows", [(s, (s - o) % n) for s in range(n)]) if o else patterns
        for o in (-2, -1, 0, 1, 2)
    ]
    offsets = jnp.stack([0 * sign_x, sign_x, sign_y, -sign_y, -sign_x]).astype(int32)
    which = (offsets[:, None] == jnp.arange(-2, 3, dtype=int32)[None, :]).astype(int32)
    near_patterns = jnp.sum(which[:, :, None, None] * jnp.stack(by_offset)[None], axis=1)
    near_patterns = near_patterns.reshape(5 * rows, slots + kept)
    near_factor_cols = near_patterns[:, :slots]
    near_product_cols = near_patterns[:, slots:]
    near_index = jnp.arange(5 * rows, dtype=int32)
    row_of, slot_of = near_index % rows, near_index // rows
    swapped = slot_of * rows + ((row_of // half_rows) ^ q) * half_rows + row_of % half_rows
    factor_at = jnp.where(slot_of == 0, near_index, swapped).astype(int32)

    columns = jnp.concatenate([margin_cols, swap(margin_cols)], axis=1)
    offset = (columns // rows - r + 2) % n - 2
    slot = jnp.sum((offset[..., None] == offsets) * jnp.arange(5, dtype=int32), axis=-1)
    picked = (slot * rows + columns % rows)[..., None] == near_index
    picked = picked.astype(int32)
    picked_cols = jnp.sum(picked[..., None] * near_factor_cols, axis=2)
    picked_at = jnp.sum(picked * factor_at, axis=2)
    my_product_cols = lax.dynamic_slice_in_dim(product_cols, q * half_kept, half_kept, 1)
    match = (picked_cols[:, None] == my_product_cols[:, :, None, None]).astype(int32)
    m_index = jnp.arange(slots, dtype=int32)
    k_index = jnp.arange(columns.shape[1], dtype=int32)
    code = k_index[:, None] * CODE + picked_at[:, None, :, None] * slots + m_index
    table, groups = packed_list(
        jnp.sum(match, axis=-1), jnp.sum(match * code, axis=-1), 5 * rows * slots
    )

    table, groups, factor_blocks, margin_blocks = lax.optimization_barrier(
        (table, groups, factor_blocks, margin_blocks)
    )
    share = half_rows * slots
    flat_factor = factor_blocks.reshape(-1, block, block)
    flat_margin = margin_blocks.reshape(-1, block, block)
    near = fetch_halo(flat_factor, lambda core: core * share, flat_margin, CHUNKS, share // CHUNKS, 0)
    moves = [(0, slice(None), 0, rows * slots)]
    for j in range(4):
        for h in range(2):
            moves.append((1, j + 4 * h, ((j + 1) * rows + h * half_rows) * slots, share))
    mine = margin_blocks.shape[1]
    lhs_moves = []
    for row in range(rows):
        lhs_moves.append((2, pl.ds(row * mine, mine), row * slots, mine))
        lhs_moves.append((1, (8, pl.ds(row * mine, mine)), row * slots + mine, mine))
    product = block_products(
        table,
        groups,
        [flat_factor, near, flat_margin],
        moves,
        lhs_moves,
        rows,
        slots,
        5 * rows * slots,
        None,
        half_kept,
    )

    targets = r * rows + jnp.arange(rows, dtype=int32)
    hit = (near_factor_cols[None] == targets[:, None, None]).astype(int32)
    held = jnp.sum(hit, axis=-1)
    near_at = rows + (slot_of - 1 + 4 * ((row_of // half_rows) ^ q)) * half_rows + row_of % half_rows
    near_at = jnp.where(slot_of == 0, near_index, near_at)
    at = jnp.sum(hit * (near_at[:, None] * slots + m_index), axis=-1)
    entry_span = 9 * rows * slots
    entry_code, _ = packed_list(held, near_index * entry_span + at, 0)
    entry_code = entry_code[:, :slots]
    entry_row, entry_at = entry_code // entry_span, entry_code % entry_span
    order = jnp.where(q == 0, near_product_cols, jnp.roll(near_product_cols, half_kept, axis=1))
    entry_pick = (entry_row[..., None] == near_index).astype(int32)
    entry_cols = jnp.sum(entry_pick[..., None] * order, axis=2)
    my_metric_cols = lax.dynamic_slice_in_dim(metric_cols, q * half_x, half_x, 1)
    match = (entry_cols[:, None] == my_metric_cols[:, :, None, None]).astype(int32)
    y_index = jnp.arange(kept, dtype=int32)
    entry_base = (entry_row // rows) * rows * kept + entry_row % rows * half_kept
    y_at = y_index // half_kept * (rows * half_kept) + y_index % half_kept
    code = m_index[:, None] * CODE + entry_base[:, None, :, None] + y_at
    table, groups = packed_list(
        jnp.sum(match, axis=-1), jnp.sum(match * code, axis=-1), 5 * rows * kept
    )

    share = rows * half_kept
    flat_product = product.reshape(-1, block, block)
    near_product = fetch_halo(
        flat_product, lambda core: 0, flat_product, CHUNKS, share // CHUNKS, 1
    )
    moves = [(0, slice(None), 0, share), (1, 8, share, share)]
    for j in range(4):
        for h in range(2):
            moves.append((1, j + 4 * h, (2 * j + 2 + h) * share, share))
    metric = block_products(
        table,
        groups,
        [flat_product, near_product, flat_factor, near.reshape(-1, block, block)],
        moves,
        [],
        rows,
        slots,
        5 * rows * kept,
        entry_at,
        half_x,
    )
    return (product, metric)


def solution(mesh):
    return jax.shard_map(
        shards,
        mesh=mesh,
        in_specs=(
            P("rows", "rep", None, None),
            P("rows", "rep"),
            P("rows", None, None, None),
            P("rows", None),
            P("rows", None),
            P("rows", None),
        ),
        out_specs=(P("rows", "rep", None, None), P("rows", "rep", None, None)),
        check_vma=False,
    )
```

```python
import jax
import jax.numpy as jnp
from jax import lax
from jax.experimental import pallas as pl
from jax.experimental.pallas import tpu as pltpu
from jax.sharding import PartitionSpec as P

MESH = pl.DeviceIdType.MESH
CHUNKS = 8
GROUP = 4
TOGETHER = 2
CODE = 1024


def fetch_halo(sent, sent_base, swapped, chunks, size, collective_id, tile=None):
    block = sent.shape[-1]
    at_x, at_y, at_z, at_second, at_swap, at_way = 0, 1, 2, 3, 8, 9

    def kernel(*refs):
        if tile is None:
            sent_ref, swapped_ref, out_ref, send_sem, recv_sem = refs
        else:
            sent_ref, swapped_ref, tile_ref, out_ref, tiles_ref, send_sem, recv_sem, tile_sem = refs
        n = lax.axis_size("rows")
        r = lax.axis_index("rows")
        q = lax.axis_index("rep")
        px, py = r % 2, (r // 2) % 2
        to_x = r + 1 - 2 * px
        to_y = r + 2 - 4 * py
        to_z = (r + n + 4 - 8 * py) % n
        from_z = (r + n - 4 + 8 * py) % n
        outer = px == py
        barrier = pltpu.get_barrier_semaphore()
        for rows, rep in ((to_x, q), (to_y, q), (from_z, q), (r, 1 - q)):
            pl.semaphore_signal(barrier, inc=1, device_id=(rows, rep), device_id_type=MESH)
        pl.semaphore_wait(barrier, 4)

        def span(c):
            return pl.ds(c * size, size)

        def copy(src, kind, place, c, target):
            return pltpu.make_async_remote_copy(
                src_ref=src,
                dst_ref=out_ref.at[place, span(c)],
                send_sem=send_sem.at[kind, c],
                recv_sem=recv_sem.at[place, c],
                device_id=target,
                device_id_type=MESH,
            )

        def own(c):
            return sent_ref.at[pl.ds(sent_base(q) + c * size, size)]

        def over_x(c):
            return copy(own(c), 0, at_x, c, (to_x, q))

        def over_y(c):
            return copy(own(c), 1, at_y, c, (to_y, q))

        def over_z(c):
            return copy(out_ref.at[at_y, span(c)], 2, at_z, c, (to_z, q))

        def second_x(c, held):
            return copy(out_ref.at[held, span(c)], 3, at_second, c, (to_x, q))

        def second_y(c):
            place = jnp.where(outer, at_second, at_way)
            return copy(out_ref.at[at_x, span(c)], 3, place, c, (to_y, q))

        def second_z(c):
            return copy(out_ref.at[at_way, span(c)], 9, at_second, c, (to_z, q))

        def share(place, c):
            return copy(out_ref.at[place, span(c)], 4 + place, 4 + place, c, (r, 1 - q))

        def own_share(c):
            return copy(swapped_ref.at[span(c)], 8, at_swap, c, (r, 1 - q))

        def arrived(place, c):
            copy(out_ref.at[place, span(c)], 0, place, c, (r, 1 - q)).wait_recv()

        def tile_copy(src, kind, place, target):
            return pltpu.make_async_remote_copy(
                src_ref=src,
                dst_ref=tiles_ref.at[place],
                send_sem=tile_sem.at[0, kind],
                recv_sem=tile_sem.at[1, place],
                device_id=target,
                device_id_type=MESH,
            )

        tile_hops = []
        if tile is not None:
            tile_hops = [
                tile_copy(tile_ref, 1, 1, (to_x, q)),
                tile_copy(tile_ref, 2, 2, (to_y, q)),
                tile_copy(tile_ref, 5, 5, (r, 1 - q)),
                tile_copy(tiles_ref.at[2], 3, 3, (to_z, q)),
            ]
            own_tile = pltpu.make_async_copy(tile_ref, tiles_ref.at[0], tile_sem.at[0, 0])
            own_tile.start()
            for tile_hop in tile_hops[:3]:
                tile_hop.start()

        pairs = [(c, c + 1) for c in range(0, chunks, 2)]
        x_order = [b for a, b in pairs] + [a for a, b in pairs]
        y_order = [a for a, b in pairs] + [b for a, b in pairs]
        ahead = 2
        for i in range(ahead):
            over_x(x_order[i]).start()
            over_y(y_order[i]).start()
        if tile is not None:
            tile_hops[1].wait_recv()
            tile_hops[3].start()
        for i in range(chunks):
            c = x_order[i]
            arrived(at_x, c)
            if c % 2:
                second_y(c).start()
            if i + ahead < chunks:
                over_x(x_order[i + ahead]).start()
            share(at_x, c).start()
            own_share(i).start()
            c = y_order[i]
            arrived(at_y, c)
            over_z(c).start()
            if c % 2 == 0:

                @pl.when(outer)
                def _(c=c):
                    second_x(c, at_y).start()

            if i + ahead < chunks:
                over_y(y_order[i + ahead]).start()
            share(at_y, c).start()
            if i >= 1:
                c = y_order[i - 1]
                arrived(at_z, c)
                if c % 2 == 0:

                    @pl.when(jnp.logical_not(outer))
                    def _(c=c):
                        second_x(c, at_z).start()

                share(at_z, c).start()
            if 1 <= i <= len(pairs):
                c = x_order[i - 1]

                @pl.when(outer)
                def _(c=c):
                    arrived(at_way, c)
                    second_z(c).start()

            if i >= len(pairs):
                for c in pairs[i - len(pairs)]:
                    arrived(at_second, c)
                    share(at_second, c).start()
        if tile is not None:
            tile_hops[3].wait_recv()

            @pl.when(outer)
            def _():
                tile_copy(tiles_ref.at[2], 4, 4, (to_x, q)).start()

            @pl.when(jnp.logical_not(outer))
            def _():
                tile_copy(tiles_ref.at[3], 4, 4, (to_x, q)).start()

            tile_hops.append(tile_copy(tiles_ref.at[2], 4, 4, (to_x, q)))
            tile_hops[4].wait_recv()
            tile_hops[0].wait_recv()
            tile_hops[2].wait_recv()
            own_tile.wait()
            for tile_hop in tile_hops:
                tile_hop.wait_send()
        c = y_order[-1]
        arrived(at_z, c)
        share(at_z, c).start()
        for c in range(chunks):
            for place in (4, 5, 6, 7, at_swap):
                arrived(place, c)
        for c in range(chunks):
            over_x(c).wait_send()
            over_y(c).wait_send()
            over_z(c).wait_send()
            second_x(c, at_z).wait_send()
            if c % 2:

                @pl.when(outer)
                def _(c=c):
                    second_z(c).wait_send()

            for place in (at_x, at_y, at_z, at_second):
                share(place, c).wait_send()
            own_share(c).wait_send()

    anywhere = pl.BlockSpec(memory_space=pl.ANY)
    out_shape = [jax.ShapeDtypeStruct((10, chunks * size, block, block), jnp.float32)]
    scratch = [pltpu.SemaphoreType.DMA((10, chunks)), pltpu.SemaphoreType.DMA((10, chunks))]
    operands = [sent, swapped]
    if tile is not None:
        out_shape.append(jax.ShapeDtypeStruct((6,) + tile.shape, tile.dtype))
        scratch.append(pltpu.SemaphoreType.DMA((2, 6)))
        operands.append(tile)
    return pl.pallas_call(
        kernel,
        out_shape=out_shape,
        in_specs=[anywhere] * len(operands),
        out_specs=[anywhere] * len(out_shape),
        scratch_shapes=scratch,
        compiler_params=pltpu.CompilerParams(collective_id=collective_id, has_side_effects=True),
    )(*operands)


def block_products(tiles, build, sources, moves, lhs_moves, rows, slots, pool_blocks, transposed, outs, n):
    block = sources[0].shape[-1]
    source_count = len(sources)

    def kernel(*refs):
        tiles_ref = refs[0]
        source_refs = refs[1 : 1 + source_count]
        out_ref, pool, lhs, high, low, sems, lhs_sems = refs[1 + source_count : 8 + source_count]
        table_ref, count_ref, where_ref, entry_ref = refs[8 + source_count :]

        def moved(index, move, target, semaphores):
            source, at, dst, count = move
            return pltpu.make_async_copy(
                source_refs[source].at[at], target.at[pl.ds(dst, count)], semaphores.at[index]
            )

        lhs_copies = [moved(i, move, lhs, lhs_sems) for i, move in enumerate(lhs_moves)]
        copies = [moved(i, move, pool, sems) for i, move in enumerate(moves)]
        for copy in lhs_copies + copies:
            copy.start()
        build_entries, build_pairs = build
        if transposed:
            build_entries(tiles_ref, entry_ref, count_ref)
            first, second = source_refs[-2:]
            bound = first.shape[0]

            def fetch(i, carry):
                code = entry_ref[i // slots * 2 * slots + i % slots] // CODE

                @pl.when(code < bound)
                def _():
                    pltpu.make_async_copy(first.at[code], lhs.at[i], lhs_sems.at[i]).start()

                @pl.when(code >= bound)
                def _():
                    pltpu.make_async_copy(
                        second.at[code - bound], lhs.at[i], lhs_sems.at[i]
                    ).start()

                return carry

            lax.fori_loop(0, rows * slots, fetch, 0)
        pool[pool_blocks] = jnp.zeros((block, block), jnp.float32)

        def clear(i, carry):
            for e in range(slots):
                table_ref[i * slots + e] = jnp.int32(pool_blocks)
            return carry

        lax.fori_loop(0, rows * outs, clear, 0)

        def forget(i, carry):
            for e in range(rows):
                where_ref[i * rows + e] = jnp.int32(outs)
            return carry

        lax.fori_loop(0, n, forget, 0)
        lax.fori_loop(
            0,
            rows,
            lambda row, carry: build_pairs(
                row, tiles_ref, table_ref, count_ref, where_ref, entry_ref
            ),
            0,
        )
        for copy in lhs_copies:
            copy.wait()

        def split(index, carry):
            for e in range(4):
                i = index * 4 + e
                if transposed:
                    pltpu.make_async_copy(source_refs[-2].at[0], lhs.at[i], lhs_sems.at[i]).wait()
                value = lhs[i].T if transposed else lhs[i]
                top = value.astype(jnp.bfloat16)
                high[i] = top
                low[i] = (value - top.astype(jnp.float32)).astype(jnp.bfloat16)
            return carry

        lax.fori_loop(0, rows * slots // 4, split, 0)
        for copy in copies:
            copy.wait()

        def term(o, g):
            row = o // outs
            left, right = [], []
            for e in range(GROUP):
                code = table_ref[o * slots + g * GROUP + e]
                s = row * slots + code // CODE
                value = pool[code % CODE]
                top = value.astype(jnp.bfloat16)
                rest = (value - top.astype(jnp.float32)).astype(jnp.bfloat16)
                left += [high[s], high[s], low[s]]
                right += [top, rest, top]
            return jnp.dot(
                jnp.concatenate(left, axis=1),
                jnp.concatenate(right, axis=0),
                preferred_element_type=jnp.float32,
            )

        def some_outputs(index, carry):
            first = index * TOGETHER
            counts = first // outs * (outs + 1) + first % outs
            steps = count_ref[counts]
            for e in range(1, TOGETHER):
                steps = jnp.maximum(steps, count_ref[counts + e])
            steps = (steps + GROUP - 1) // GROUP

            def one_group(g, totals):
                return tuple(totals[e] + term(first + e, g) for e in range(TOGETHER))

            zero = jnp.zeros((block, block), jnp.float32)
            totals = lax.fori_loop(0, steps, one_group, (zero,) * TOGETHER)
            for e in range(TOGETHER):
                out_ref[first + e] = totals[e]
            return carry

        lax.fori_loop(0, rows * outs // TOGETHER, some_outputs, 0)

    in_specs = (
        [pl.BlockSpec(memory_space=pltpu.SMEM)]
        + [pl.BlockSpec(memory_space=pl.ANY)] * source_count
    )
    result = pl.pallas_call(
        kernel,
        out_shape=jax.ShapeDtypeStruct((rows * outs, block, block), jnp.float32),
        in_specs=in_specs,
        out_specs=pl.BlockSpec(memory_space=pltpu.VMEM),
        scratch_shapes=[
            pltpu.VMEM((pool_blocks + 1, block, block), jnp.float32),
            pltpu.VMEM((rows * slots, block, block), jnp.float32),
            pltpu.VMEM((rows * slots, block, block), jnp.bfloat16),
            pltpu.VMEM((rows * slots, block, block), jnp.bfloat16),
            pltpu.SemaphoreType.DMA((len(moves),)),
            pltpu.SemaphoreType.DMA((rows * slots,)),
            pltpu.SMEM((rows * outs * slots + 2048,), jnp.int32),
            pltpu.SMEM((rows * (outs + 1) + 8,), jnp.int32),
            pltpu.SMEM((n * rows,), jnp.int32),
            pltpu.SMEM((rows * 2 * slots + 1024,), jnp.int32),
        ],
        compiler_params=pltpu.CompilerParams(vmem_limit_bytes=52 * 1024 * 1024),
        cost_estimate=pl.CostEstimate(
            flops=rows * outs * 10 * 6 * block**3 * 4,
            bytes_accessed=(pool_blocks + rows * (slots + outs)) * block * block * 4,
            transcendentals=0,
        ),
    )(tiles, *sources)
    return result.reshape(rows, outs, block, block)


def shards(margin_blocks, margin_cols, factor_blocks, factor_cols, product_cols, metric_cols):
    rows, slots, block = factor_blocks.shape[:3]
    kept, kept_x = product_cols.shape[1], metric_cols.shape[1]
    half_rows, half_kept, half_x = rows // 2, kept // 2, kept_x // 2
    n = lax.axis_size("rows")
    r = lax.axis_index("rows")
    q = lax.axis_index("rep")
    mine = margin_blocks.shape[1]
    at_kept, at_margin = slots, slots + kept
    at_metric = at_margin + mine
    at_place = at_metric + kept_x
    ones = jnp.ones((rows, 1), jnp.int32)
    tile = jnp.concatenate(
        [factor_cols, product_cols, margin_cols, metric_cols, r * ones, q * ones], axis=1
    )
    tile = jnp.pad(tile, ((0, 8 - rows), (0, 128 - tile.shape[1])))

    def place_of(tiles):
        return tiles[0, 0, at_place], tiles[0, 0, at_place + 1]

    def append(row, out, code, outs, table, counts):
        count = counts[row * (outs + 1) + out]
        start = jnp.where(out == outs, rows * outs, row * outs + out)
        table[start * slots + count] = code
        counts[row * (outs + 1) + out] = count + 1

    def product_pairs(row, tiles, table, counts, where, entry):
        mr, mq = place_of(tiles)
        sign_x = 1 - 2 * (mr % 2)
        sign_y = 2 - 4 * (mr // 2 % 2)
        for y in range(half_kept):
            where[tiles[0, row, at_kept + mq * half_kept + y]] = jnp.int32(y)
        for y in range(half_kept + 1):
            counts[row * (half_kept + 1) + y] = jnp.int32(0)

        def one_margin(k, carry):
            theirs = k // mine
            column = tiles[5 * theirs, row, at_margin + k % mine]
            offset = (column // rows - mr + 2 + n) % n - 2
            slot = jnp.where(offset == sign_x, 1, jnp.where(offset == sign_y, 2, 3))
            slot = jnp.where(offset == -sign_x, 4, jnp.where(offset == 0, 0, slot))
            inner = column % rows
            swapped = ((inner // half_rows) ^ mq) * half_rows + inner % half_rows
            base = k * CODE + (slot * rows + jnp.where(slot == 0, inner, swapped)) * slots
            for m in range(slots):
                out = where[tiles[slot, inner, m]]
                append(row, out, base + m, half_kept, table, counts)
            return carry

        lax.fori_loop(0, 2 * mine, one_margin, 0)
        for y in range(half_kept):
            where[tiles[0, row, at_kept + mq * half_kept + y]] = jnp.int32(half_kept)
        return 0

    def metric_entries(tiles, entry, counts):
        mr, mq = place_of(tiles)
        for a in range(rows + 1):
            counts[a] = jnp.int32(0)

        def one_row(near_row, carry):
            slot, inner = near_row // rows, near_row % rows
            other = (inner // half_rows) ^ mq
            held = rows + (slot - 1 + 4 * other) * half_rows + inner % half_rows
            base = jnp.where(slot == 0, inner, held) * slots
            for m in range(slots):
                a = tiles[slot, inner, m] - mr * rows
                a = jnp.where((a >= 0) & (a < rows), a, rows)
                count = counts[a]
                entry[a * 2 * slots + count] = (base + m) * CODE + near_row
                counts[a] = count + 1
            return carry

        lax.fori_loop(0, 5 * rows, one_row, 0)

    def metric_pairs(row, tiles, table, counts, where, entry):
        mr, mq = place_of(tiles)
        for x in range(half_x):
            where[tiles[0, row, at_metric + mq * half_x + x]] = jnp.int32(x)
        for x in range(half_x + 1):
            counts[row * (half_x + 1) + x] = jnp.int32(0)

        def one_entry(t, carry):
            near_row = entry[row * 2 * slots + t] % CODE
            slot, inner = near_row // rows, near_row % rows
            for h in range(2):
                base = ((2 * slot + (h ^ mq)) * rows + inner) * half_kept + t * CODE
                for y in range(half_kept):
                    out = where[tiles[slot, inner, at_kept + h * half_kept + y]]
                    append(row, out, base + y, half_x, table, counts)
            return carry

        lax.fori_loop(0, slots, one_entry, 0)
        for x in range(half_x):
            where[tiles[0, row, at_metric + mq * half_x + x]] = jnp.int32(half_x)
        return 0

    share = half_rows * slots
    flat_factor = factor_blocks.reshape(-1, block, block)
    flat_margin = margin_blocks.reshape(-1, block, block)
    near, tiles = fetch_halo(
        flat_factor, lambda core: core * share, flat_margin, CHUNKS, share // CHUNKS, 0, tile
    )
    moves = [(0, slice(None), 0, rows * slots)]
    for j in range(4):
        for h in range(2):
            moves.append((1, j + 4 * h, ((j + 1) * rows + h * half_rows) * slots, share))
    lhs_moves = []
    for row in range(rows):
        lhs_moves.append((2, pl.ds(row * mine, mine), row * slots, mine))
        lhs_moves.append((1, (8, pl.ds(row * mine, mine)), row * slots + mine, mine))
    product = block_products(
        tiles,
        (None, product_pairs),
        [flat_factor, near, flat_margin],
        moves,
        lhs_moves,
        rows,
        slots,
        5 * rows * slots,
        False,
        half_kept,
        n,
    )

    share = rows * half_kept
    flat_product = product.reshape(-1, block, block)
    (near_product,) = fetch_halo(
        flat_product, lambda core: 0, flat_product, CHUNKS, share // CHUNKS, 1
    )
    moves = [(0, slice(None), 0, share), (1, 8, share, share)]
    for j in range(4):
        for h in range(2):
            moves.append((1, j + 4 * h, (2 * j + 2 + h) * share, share))
    metric = block_products(
        tiles,
        (metric_entries, metric_pairs),
        [flat_product, near_product, flat_factor, near.reshape(-1, block, block)],
        moves,
        [],
        rows,
        slots,
        5 * rows * kept,
        True,
        half_x,
        n,
    )
    return (product, metric)


def solution(mesh):
    return jax.shard_map(
        shards,
        mesh=mesh,
        in_specs=(
            P("rows", "rep", None, None),
            P("rows", "rep"),
            P("rows", None, None, None),
            P("rows", None),
            P("rows", None),
            P("rows", None),
        ),
        out_specs=(P("rows", "rep", None, None), P("rows", "rep", None, None)),
        check_vma=False,
    )
```

```python
import jax
import jax.numpy as jnp
from jax import lax
from jax.experimental import pallas as pl
from jax.experimental.pallas import tpu as pltpu
from jax.sharding import PartitionSpec as P

MESH = pl.DeviceIdType.MESH
CHUNKS = 8
GROUP = 4
TOGETHER = 4
CODE = 1024


def fetch_halo(sent, sent_base, swapped, chunks, size, collective_id, tile=None):
    block = sent.shape[-1]
    at_x, at_y, at_z, at_second, at_swap, at_way = 0, 1, 2, 3, 8, 9

    def kernel(*refs):
        if tile is None:
            sent_ref, swapped_ref, out_ref, send_sem, recv_sem = refs
        else:
            sent_ref, swapped_ref, tile_ref, out_ref, tiles_ref, send_sem, recv_sem, tile_sem = refs
        n = lax.axis_size("rows")
        r = lax.axis_index("rows")
        q = lax.axis_index("rep")
        px, py = r % 2, (r // 2) % 2
        to_x = r + 1 - 2 * px
        to_y = r + 2 - 4 * py
        to_z = (r + n + 4 - 8 * py) % n
        from_z = (r + n - 4 + 8 * py) % n
        outer = px == py
        barrier = pltpu.get_barrier_semaphore()
        for rows, rep in ((to_x, q), (to_y, q), (from_z, q), (r, 1 - q)):
            pl.semaphore_signal(barrier, inc=1, device_id=(rows, rep), device_id_type=MESH)
        pl.semaphore_wait(barrier, 4)

        def span(c):
            return pl.ds(c * size, size)

        def copy(src, kind, place, c, target):
            return pltpu.make_async_remote_copy(
                src_ref=src,
                dst_ref=out_ref.at[place, span(c)],
                send_sem=send_sem.at[kind, c],
                recv_sem=recv_sem.at[place, c],
                device_id=target,
                device_id_type=MESH,
            )

        def own(c):
            return sent_ref.at[pl.ds(sent_base(q) + c * size, size)]

        def over_x(c):
            return copy(own(c), 0, at_x, c, (to_x, q))

        def over_y(c):
            return copy(own(c), 1, at_y, c, (to_y, q))

        def over_z(c):
            return copy(out_ref.at[at_y, span(c)], 2, at_z, c, (to_z, q))

        def second_x(c, held):
            return copy(out_ref.at[held, span(c)], 3, at_second, c, (to_x, q))

        def second_y(c):
            place = jnp.where(outer, at_second, at_way)
            return copy(out_ref.at[at_x, span(c)], 3, place, c, (to_y, q))

        def second_z(c):
            return copy(out_ref.at[at_way, span(c)], 9, at_second, c, (to_z, q))

        def share(place, c):
            return copy(out_ref.at[place, span(c)], 4 + place, 4 + place, c, (r, 1 - q))

        def own_share(c):
            return copy(swapped_ref.at[span(c)], 8, at_swap, c, (r, 1 - q))

        def arrived(place, c):
            copy(out_ref.at[place, span(c)], 0, place, c, (r, 1 - q)).wait_recv()

        def tile_copy(src, kind, place, target):
            return pltpu.make_async_remote_copy(
                src_ref=src,
                dst_ref=tiles_ref.at[place],
                send_sem=tile_sem.at[0, kind],
                recv_sem=tile_sem.at[1, place],
                device_id=target,
                device_id_type=MESH,
            )

        tile_hops = []
        if tile is not None:
            tile_hops = [
                tile_copy(tile_ref, 1, 1, (to_x, q)),
                tile_copy(tile_ref, 2, 2, (to_y, q)),
                tile_copy(tile_ref, 5, 5, (r, 1 - q)),
                tile_copy(tiles_ref.at[2], 3, 3, (to_z, q)),
            ]
            own_tile = pltpu.make_async_copy(tile_ref, tiles_ref.at[0], tile_sem.at[0, 0])
            own_tile.start()
            for tile_hop in tile_hops[:3]:
                tile_hop.start()

        pairs = [(c, c + 1) for c in range(0, chunks, 2)]
        x_order = [b for a, b in pairs] + [a for a, b in pairs]
        y_order = [a for a, b in pairs] + [b for a, b in pairs]
        ahead = 2
        for i in range(ahead):
            over_x(x_order[i]).start()
            over_y(y_order[i]).start()
        if tile is not None:
            tile_hops[1].wait_recv()
            tile_hops[3].start()
        for i in range(chunks):
            c = x_order[i]
            arrived(at_x, c)
            if c % 2:
                second_y(c).start()
            if i + ahead < chunks:
                over_x(x_order[i + ahead]).start()
            share(at_x, c).start()
            own_share(i).start()
            c = y_order[i]
            arrived(at_y, c)
            over_z(c).start()
            if c % 2 == 0:

                @pl.when(outer)
                def _(c=c):
                    second_x(c, at_y).start()

            if i + ahead < chunks:
                over_y(y_order[i + ahead]).start()
            share(at_y, c).start()
            if i >= 1:
                c = y_order[i - 1]
                arrived(at_z, c)
                if c % 2 == 0:

                    @pl.when(jnp.logical_not(outer))
                    def _(c=c):
                        second_x(c, at_z).start()

                share(at_z, c).start()
            if 1 <= i <= len(pairs):
                c = x_order[i - 1]

                @pl.when(outer)
                def _(c=c):
                    arrived(at_way, c)
                    second_z(c).start()

            if i >= len(pairs):
                for c in pairs[i - len(pairs)]:
                    arrived(at_second, c)
                    share(at_second, c).start()
        if tile is not None:
            tile_hops[3].wait_recv()

            @pl.when(outer)
            def _():
                tile_copy(tiles_ref.at[2], 4, 4, (to_x, q)).start()

            @pl.when(jnp.logical_not(outer))
            def _():
                tile_copy(tiles_ref.at[3], 4, 4, (to_x, q)).start()

            tile_hops.append(tile_copy(tiles_ref.at[2], 4, 4, (to_x, q)))
            tile_hops[4].wait_recv()
            tile_hops[0].wait_recv()
            tile_hops[2].wait_recv()
            own_tile.wait()
            for tile_hop in tile_hops:
                tile_hop.wait_send()
        c = y_order[-1]
        arrived(at_z, c)
        share(at_z, c).start()
        for c in range(chunks):
            for place in (4, 5, 6, 7, at_swap):
                arrived(place, c)
        for c in range(chunks):
            over_x(c).wait_send()
            over_y(c).wait_send()
            over_z(c).wait_send()
            second_x(c, at_z).wait_send()
            if c % 2:

                @pl.when(outer)
                def _(c=c):
                    second_z(c).wait_send()

            for place in (at_x, at_y, at_z, at_second):
                share(place, c).wait_send()
            own_share(c).wait_send()

    anywhere = pl.BlockSpec(memory_space=pl.ANY)
    out_shape = [jax.ShapeDtypeStruct((10, chunks * size, block, block), jnp.float32)]
    scratch = [pltpu.SemaphoreType.DMA((10, chunks)), pltpu.SemaphoreType.DMA((10, chunks))]
    operands = [sent, swapped]
    if tile is not None:
        out_shape.append(jax.ShapeDtypeStruct((6,) + tile.shape, tile.dtype))
        scratch.append(pltpu.SemaphoreType.DMA((2, 6)))
        operands.append(tile)
    return pl.pallas_call(
        kernel,
        out_shape=out_shape,
        in_specs=[anywhere] * len(operands),
        out_specs=[anywhere] * len(out_shape),
        scratch_shapes=scratch,
        compiler_params=pltpu.CompilerParams(collective_id=collective_id, has_side_effects=True),
    )(*operands)


def block_products(tiles, build, sources, moves, lhs_moves, rows, slots, pool_blocks, transposed, outs, n):
    block = sources[0].shape[-1]
    source_count = len(sources)

    def kernel(*refs):
        tiles_ref = refs[0]
        source_refs = refs[1 : 1 + source_count]
        out_ref, pool, lhs, high, low, sems, lhs_sems = refs[1 + source_count : 8 + source_count]
        table_ref, count_ref, where_ref, entry_ref = refs[8 + source_count :]

        def moved(index, move, target, semaphores):
            source, at, dst, count = move
            return pltpu.make_async_copy(
                source_refs[source].at[at], target.at[pl.ds(dst, count)], semaphores.at[index]
            )

        lhs_copies = [moved(i, move, lhs, lhs_sems) for i, move in enumerate(lhs_moves)]
        copies = [moved(i, move, pool, sems) for i, move in enumerate(moves)]
        for copy in lhs_copies + copies:
            copy.start()
        total = n * rows

        def clear(i, carry):
            for e in range(slots):
                table_ref[i * slots + e] = jnp.int32(pool_blocks)
            return carry

        lax.fori_loop(0, rows * outs, clear, 0)

        def forget(i, carry):
            for e in range(16):
                where_ref[i * 16 + e] = jnp.int32(pool_blocks)
            return carry

        lax.fori_loop(0, 5 * rows * total // 16, forget, 0)
        place_rows, entries, base_of, column_of = build
        if transposed:
            entries(tiles_ref, where_ref, entry_ref, pool_blocks)
            first, second = source_refs[-2:]
            bound = first.shape[0]

            def fetch(i, carry):
                code = entry_ref[i // slots * 2 * slots + i % slots] // CODE

                @pl.when(code < bound)
                def _():
                    pltpu.make_async_copy(first.at[code], lhs.at[i], lhs_sems.at[i]).start()

                @pl.when(code >= bound)
                def _():
                    pltpu.make_async_copy(
                        second.at[code - bound], lhs.at[i], lhs_sems.at[i]
                    ).start()

                return carry

            lax.fori_loop(0, rows * slots, fetch, 0)
        pool[pool_blocks] = jnp.zeros((block, block), jnp.float32)

        place_rows(tiles_ref, where_ref)

        def list_row(row, carry):
            bases = [base_of(tiles_ref, entry_ref, row, e) * total for e in range(slots)]

            def list_output(o, carry):
                column = column_of(tiles_ref, row, o)
                start = (row * outs + o) * slots
                count = jnp.int32(0)
                for e in range(slots):
                    at = where_ref[bases[e] + column]
                    table_ref[start + count] = at + e * CODE
                    count = count + jnp.where(at != pool_blocks, 1, 0)
                count_ref[row * outs + o] = count
                return carry

            return lax.fori_loop(0, outs, list_output, carry)

        lax.fori_loop(0, rows, list_row, 0)
        for copy in lhs_copies:
            copy.wait()

        def split(index, carry):
            for e in range(4):
                i = index * 4 + e
                if transposed:
                    pltpu.make_async_copy(source_refs[-2].at[0], lhs.at[i], lhs_sems.at[i]).wait()
                value = lhs[i].T if transposed else lhs[i]
                top = value.astype(jnp.bfloat16)
                high[i] = top
                low[i] = (value - top.astype(jnp.float32)).astype(jnp.bfloat16)
            return carry

        lax.fori_loop(0, rows * slots // 4, split, 0)
        for copy in copies:
            copy.wait()

        def term(o, g):
            row = o // outs
            left, right = [], []
            for e in range(GROUP):
                code = table_ref[o * slots + g * GROUP + e]
                s = row * slots + code // CODE
                value = pool[code % CODE]
                top = value.astype(jnp.bfloat16)
                rest = (value - top.astype(jnp.float32)).astype(jnp.bfloat16)
                left += [high[s], high[s], low[s]]
                right += [top, rest, top]
            return jnp.dot(
                jnp.concatenate(left, axis=1),
                jnp.concatenate(right, axis=0),
                preferred_element_type=jnp.float32,
            )

        def some_outputs(index, carry):
            first = index * TOGETHER
            steps = count_ref[first]
            for e in range(1, TOGETHER):
                steps = jnp.maximum(steps, count_ref[first + e])
            steps = (steps + GROUP - 1) // GROUP

            def one_group(g, totals):
                return tuple(totals[e] + term(first + e, g) for e in range(TOGETHER))

            zero = jnp.zeros((block, block), jnp.float32)
            totals = lax.fori_loop(0, steps, one_group, (zero,) * TOGETHER)
            for e in range(TOGETHER):
                out_ref[first + e] = totals[e]
            return carry

        lax.fori_loop(0, rows * outs // TOGETHER, some_outputs, 0)

    in_specs = (
        [pl.BlockSpec(memory_space=pltpu.SMEM)]
        + [pl.BlockSpec(memory_space=pl.ANY)] * source_count
    )
    result = pl.pallas_call(
        kernel,
        out_shape=jax.ShapeDtypeStruct((rows * outs, block, block), jnp.float32),
        in_specs=in_specs,
        out_specs=pl.BlockSpec(memory_space=pltpu.VMEM),
        scratch_shapes=[
            pltpu.VMEM((pool_blocks + 1, block, block), jnp.float32),
            pltpu.VMEM((rows * slots, block, block), jnp.float32),
            pltpu.VMEM((rows * slots, block, block), jnp.bfloat16),
            pltpu.VMEM((rows * slots, block, block), jnp.bfloat16),
            pltpu.SemaphoreType.DMA((len(moves),)),
            pltpu.SemaphoreType.DMA((rows * slots,)),
            pltpu.SMEM((rows * outs * slots,), jnp.int32),
            pltpu.SMEM((rows * outs,), jnp.int32),
            pltpu.SMEM((5 * rows * n * rows,), jnp.int32),
            pltpu.SMEM((rows * 2 * slots,), jnp.int32),
        ],
        compiler_params=pltpu.CompilerParams(vmem_limit_bytes=52 * 1024 * 1024),
        cost_estimate=pl.CostEstimate(
            flops=rows * outs * 10 * 6 * block**3 * 4,
            bytes_accessed=(pool_blocks + rows * (slots + outs)) * block * block * 4,
            transcendentals=0,
        ),
    )(tiles, *sources)
    return result.reshape(rows, outs, block, block)


def shards(margin_blocks, margin_cols, factor_blocks, factor_cols, product_cols, metric_cols):
    rows, slots, block = factor_blocks.shape[:3]
    kept, kept_x = product_cols.shape[1], metric_cols.shape[1]
    half_rows, half_kept, half_x = rows // 2, kept // 2, kept_x // 2
    n = lax.axis_size("rows")
    r = lax.axis_index("rows")
    q = lax.axis_index("rep")
    total = n * rows
    mine = margin_blocks.shape[1]
    at_kept, at_margin = slots, slots + kept
    at_metric = at_margin + mine
    at_place = at_metric + kept_x
    ones = jnp.ones((rows, 1), jnp.int32)
    tile = jnp.concatenate(
        [factor_cols, product_cols, margin_cols, metric_cols, r * ones, q * ones], axis=1
    )
    tile = jnp.pad(tile, ((0, 8 - rows), (0, 128 - tile.shape[1])))

    def place_of(tiles):
        return tiles[0, 0, at_place], tiles[0, 0, at_place + 1]

    def place_factor(tiles, where):
        _, mq = place_of(tiles)

        def one_row(near_row, carry):
            slot, inner = near_row // rows, near_row % rows
            swapped = ((inner // half_rows) ^ mq) * half_rows + inner % half_rows
            base = (slot * rows + jnp.where(slot == 0, inner, swapped)) * slots
            for m in range(slots):
                where[near_row * total + tiles[slot, inner, m]] = base + m
            return carry

        lax.fori_loop(0, 5 * rows, one_row, 0)

    def margin_row(tiles, entry, row, k):
        mr, _ = place_of(tiles)
        sign_x = 1 - 2 * (mr % 2)
        sign_y = 2 - 4 * (mr // 2 % 2)
        column = tiles[5 * (k // mine), row, at_margin + k % mine]
        offset = (column // rows - mr + 2 + n) % n - 2
        slot = jnp.where(offset == sign_x, 1, jnp.where(offset == sign_y, 2, 3))
        slot = jnp.where(offset == -sign_x, 4, jnp.where(offset == 0, 0, slot))
        return slot * rows + column % rows

    def product_column(tiles, row, y):
        return tiles[0, row, at_kept + place_of(tiles)[1] * half_kept + y]

    def metric_entries(tiles, where, entry, missing):
        mr, mq = place_of(tiles)

        def each_block(visit):
            def one_row(near_row, carry):
                slot, inner = near_row // rows, near_row % rows
                other = (inner // half_rows) ^ mq
                held = rows + (slot - 1 + 4 * other) * half_rows + inner % half_rows
                base = jnp.where(slot == 0, inner, held) * slots
                for m in range(slots):
                    where[near_row * total + tiles[slot, inner, m]] = visit(base + m)
                return carry

            lax.fori_loop(0, 5 * rows, one_row, 0)

        each_block(lambda at: at + missing + 1)

        def one_column(a, carry):
            count = jnp.int32(0)
            for near_row in range(5 * rows):
                at = where[near_row * total + mr * rows + a]
                entry[a * 2 * slots + count] = (at - missing - 1) * CODE + near_row
                count = count + jnp.where(at != missing, 1, 0)
            return carry

        lax.fori_loop(0, rows, one_column, 0)
        each_block(lambda at: jnp.int32(missing))

    def place_product(tiles, where):
        _, mq = place_of(tiles)

        def one_row(near_row, carry):
            slot, inner = near_row // rows, near_row % rows
            for h in range(2):
                base = ((2 * slot + (h ^ mq)) * rows + inner) * half_kept
                for y in range(half_kept):
                    column = tiles[slot, inner, at_kept + h * half_kept + y]
                    where[near_row * total + column] = base + y
            return carry

        lax.fori_loop(0, 5 * rows, one_row, 0)

    def entry_row(tiles, entry, row, t):
        return entry[row * 2 * slots + t] % CODE

    def metric_column(tiles, row, x):
        return tiles[0, row, at_metric + place_of(tiles)[1] * half_x + x]

    share = half_rows * slots
    flat_factor = factor_blocks.reshape(-1, block, block)
    flat_margin = margin_blocks.reshape(-1, block, block)
    near, tiles = fetch_halo(
        flat_factor, lambda core: core * share, flat_margin, CHUNKS, share // CHUNKS, 0, tile
    )
    moves = [(0, slice(None), 0, rows * slots)]
    for j in range(4):
        for h in range(2):
            moves.append((1, j + 4 * h, ((j + 1) * rows + h * half_rows) * slots, share))
    lhs_moves = []
    for row in range(rows):
        lhs_moves.append((2, pl.ds(row * mine, mine), row * slots, mine))
        lhs_moves.append((1, (8, pl.ds(row * mine, mine)), row * slots + mine, mine))
    product = block_products(
        tiles,
        (place_factor, None, margin_row, product_column),
        [flat_factor, near, flat_margin],
        moves,
        lhs_moves,
        rows,
        slots,
        5 * rows * slots,
        False,
        half_kept,
        n,
    )

    share = rows * half_kept
    flat_product = product.reshape(-1, block, block)
    (near_product,) = fetch_halo(
        flat_product, lambda core: 0, flat_product, CHUNKS, share // CHUNKS, 1
    )
    moves = [(0, slice(None), 0, share), (1, 8, share, share)]
    for j in range(4):
        for h in range(2):
            moves.append((1, j + 4 * h, (2 * j + 2 + h) * share, share))
    metric = block_products(
        tiles,
        (place_product, metric_entries, entry_row, metric_column),
        [flat_product, near_product, flat_factor, near.reshape(-1, block, block)],
        moves,
        [],
        rows,
        slots,
        5 * rows * kept,
        True,
        half_x,
        n,
    )
    return (product, metric)


def solution(mesh):
    return jax.shard_map(
        shards,
        mesh=mesh,
        in_specs=(
            P("rows", "rep", None, None),
            P("rows", "rep"),
            P("rows", None, None, None),
            P("rows", None),
            P("rows", None),
            P("rows", None),
        ),
        out_specs=(P("rows", "rep", None, None), P("rows", "rep", None, None)),
        check_vma=False,
    )
```

```python
import jax
import jax.numpy as jnp
from jax import lax
from jax.experimental import pallas as pl
from jax.experimental.pallas import tpu as pltpu
from jax.sharding import PartitionSpec as P

MESH = pl.DeviceIdType.MESH
CHUNKS = 16
GROUP = 4
TOGETHER = 4
CODE = 1024


def fetch_halo(sent, sent_base, swapped, chunks, size, collective_id, tile=None):
    block = sent.shape[-1]
    at_x, at_y, at_z, at_second, at_swap, at_way = 0, 1, 2, 3, 8, 9

    def kernel(*refs):
        if tile is None:
            sent_ref, swapped_ref, out_ref, send_sem, recv_sem = refs
        else:
            sent_ref, swapped_ref, tile_ref, out_ref, tiles_ref, send_sem, recv_sem, tile_sem = refs
        n = lax.axis_size("rows")
        r = lax.axis_index("rows")
        q = lax.axis_index("rep")
        px, py = r % 2, (r // 2) % 2
        to_x = r + 1 - 2 * px
        to_y = r + 2 - 4 * py
        to_z = (r + n + 4 - 8 * py) % n
        from_z = (r + n - 4 + 8 * py) % n
        outer = px == py
        barrier = pltpu.get_barrier_semaphore()
        for rows, rep in ((to_x, q), (to_y, q), (from_z, q), (r, 1 - q)):
            pl.semaphore_signal(barrier, inc=1, device_id=(rows, rep), device_id_type=MESH)
        pl.semaphore_wait(barrier, 4)

        def span(c):
            return pl.ds(c * size, size)

        def copy(src, kind, place, c, target):
            return pltpu.make_async_remote_copy(
                src_ref=src,
                dst_ref=out_ref.at[place, span(c)],
                send_sem=send_sem.at[kind, c],
                recv_sem=recv_sem.at[place, c],
                device_id=target,
                device_id_type=MESH,
            )

        def own(c):
            return sent_ref.at[pl.ds(sent_base(q) + c * size, size)]

        def over_x(c):
            return copy(own(c), 0, at_x, c, (to_x, q))

        def over_y(c):
            return copy(own(c), 1, at_y, c, (to_y, q))

        def over_z(c):
            return copy(out_ref.at[at_y, span(c)], 2, at_z, c, (to_z, q))

        def second_x(c, held):
            return copy(out_ref.at[held, span(c)], 3, at_second, c, (to_x, q))

        def second_y(c):
            place = jnp.where(outer, at_second, at_way)
            return copy(out_ref.at[at_x, span(c)], 3, place, c, (to_y, q))

        def second_z(c):
            return copy(out_ref.at[at_way, span(c)], 9, at_second, c, (to_z, q))

        def share(place, c):
            return copy(out_ref.at[place, span(c)], 4 + place, 4 + place, c, (r, 1 - q))

        def own_share(c):
            return copy(swapped_ref.at[span(c)], 8, at_swap, c, (r, 1 - q))

        def arrived(place, c):
            copy(out_ref.at[place, span(c)], 0, place, c, (r, 1 - q)).wait_recv()

        def tile_copy(src, kind, place, target):
            return pltpu.make_async_remote_copy(
                src_ref=src,
                dst_ref=tiles_ref.at[place],
                send_sem=tile_sem.at[0, kind],
                recv_sem=tile_sem.at[1, place],
                device_id=target,
                device_id_type=MESH,
            )

        tile_hops = []
        if tile is not None:
            tile_hops = [
                tile_copy(tile_ref, 1, 1, (to_x, q)),
                tile_copy(tile_ref, 2, 2, (to_y, q)),
                tile_copy(tile_ref, 5, 5, (r, 1 - q)),
                tile_copy(tiles_ref.at[2], 3, 3, (to_z, q)),
            ]
            own_tile = pltpu.make_async_copy(tile_ref, tiles_ref.at[0], tile_sem.at[0, 0])
            own_tile.start()
            for tile_hop in tile_hops[:3]:
                tile_hop.start()

        pairs = [(c, c + 1) for c in range(0, chunks, 2)]
        x_order = [b for a, b in pairs] + [a for a, b in pairs]
        y_order = [a for a, b in pairs] + [b for a, b in pairs]
        ahead = chunks // 4
        for i in range(ahead):
            over_x(x_order[i]).start()
            over_y(y_order[i]).start()
        if tile is not None:
            tile_hops[1].wait_recv()
            tile_hops[3].start()
        for i in range(chunks):
            c = x_order[i]
            arrived(at_x, c)
            if c % 2:
                second_y(c).start()
            if i + ahead < chunks:
                over_x(x_order[i + ahead]).start()
            share(at_x, c).start()
            own_share(i).start()
            c = y_order[i]
            arrived(at_y, c)
            over_z(c).start()
            if c % 2 == 0:

                @pl.when(outer)
                def _(c=c):
                    second_x(c, at_y).start()

            if i + ahead < chunks:
                over_y(y_order[i + ahead]).start()
            share(at_y, c).start()
            if i >= 1:
                c = y_order[i - 1]
                arrived(at_z, c)
                if c % 2 == 0:

                    @pl.when(jnp.logical_not(outer))
                    def _(c=c):
                        second_x(c, at_z).start()

                share(at_z, c).start()
            if 1 <= i <= len(pairs):
                c = x_order[i - 1]

                @pl.when(outer)
                def _(c=c):
                    arrived(at_way, c)
                    second_z(c).start()

            if i >= len(pairs):
                for c in pairs[i - len(pairs)]:
                    arrived(at_second, c)
                    share(at_second, c).start()
        if tile is not None:
            tile_hops[3].wait_recv()

            @pl.when(outer)
            def _():
                tile_copy(tiles_ref.at[2], 4, 4, (to_x, q)).start()

            @pl.when(jnp.logical_not(outer))
            def _():
                tile_copy(tiles_ref.at[3], 4, 4, (to_x, q)).start()

            tile_hops.append(tile_copy(tiles_ref.at[2], 4, 4, (to_x, q)))
            tile_hops[4].wait_recv()
            tile_hops[0].wait_recv()
            tile_hops[2].wait_recv()
            own_tile.wait()
            for tile_hop in tile_hops:
                tile_hop.wait_send()
        c = y_order[-1]
        arrived(at_z, c)
        share(at_z, c).start()
        for c in range(chunks):
            for place in (4, 5, 6, 7, at_swap):
                arrived(place, c)
        for c in range(chunks):
            over_x(c).wait_send()
            over_y(c).wait_send()
            over_z(c).wait_send()
            second_x(c, at_z).wait_send()
            if c % 2:

                @pl.when(outer)
                def _(c=c):
                    second_z(c).wait_send()

            for place in (at_x, at_y, at_z, at_second):
                share(place, c).wait_send()
            own_share(c).wait_send()

    anywhere = pl.BlockSpec(memory_space=pl.ANY)
    out_shape = [jax.ShapeDtypeStruct((10, chunks * size, block, block), jnp.float32)]
    scratch = [pltpu.SemaphoreType.DMA((10, chunks)), pltpu.SemaphoreType.DMA((10, chunks))]
    operands = [sent, swapped]
    if tile is not None:
        out_shape.append(jax.ShapeDtypeStruct((6,) + tile.shape, tile.dtype))
        scratch.append(pltpu.SemaphoreType.DMA((2, 6)))
        operands.append(tile)
    return pl.pallas_call(
        kernel,
        out_shape=out_shape,
        in_specs=[anywhere] * len(operands),
        out_specs=[anywhere] * len(out_shape),
        scratch_shapes=scratch,
        compiler_params=pltpu.CompilerParams(collective_id=collective_id, has_side_effects=True),
    )(*operands)


def block_products(tiles, build, sources, moves, lhs_moves, rows, slots, pool_blocks, transposed, outs, n):
    block = sources[0].shape[-1]
    source_count = len(sources)

    def kernel(*refs):
        tiles_ref = refs[0]
        source_refs = refs[1 : 1 + source_count]
        out_ref, pool, lhs, high, low, sems, lhs_sems = refs[1 + source_count : 8 + source_count]
        table_ref, count_ref, where_ref, entry_ref = refs[8 + source_count :]

        def moved(index, move, target, semaphores):
            source, at, dst, count = move
            return pltpu.make_async_copy(
                source_refs[source].at[at], target.at[pl.ds(dst, count)], semaphores.at[index]
            )

        lhs_copies = [moved(i, move, lhs, lhs_sems) for i, move in enumerate(lhs_moves)]
        copies = [moved(i, move, pool, sems) for i, move in enumerate(moves)]
        for copy in lhs_copies + copies:
            copy.start()
        total = n * rows

        def clear(i, carry):
            for e in range(slots):
                table_ref[i * slots + e] = jnp.int32(pool_blocks)
            return carry

        lax.fori_loop(0, rows * outs, clear, 0)

        def forget(i, carry):
            for e in range(16):
                where_ref[i * 16 + e] = jnp.int32(pool_blocks)
            return carry

        lax.fori_loop(0, 5 * rows * total // 16, forget, 0)
        place_rows, entries, base_of, column_of = build
        if transposed:
            entries(tiles_ref, where_ref, entry_ref, pool_blocks)
            first, second = source_refs[-2:]
            bound = first.shape[0]

            def fetch(i, carry):
                code = entry_ref[i // slots * 2 * slots + i % slots] // CODE

                @pl.when(code < bound)
                def _():
                    pltpu.make_async_copy(first.at[code], lhs.at[i], lhs_sems.at[i]).start()

                @pl.when(code >= bound)
                def _():
                    pltpu.make_async_copy(
                        second.at[code - bound], lhs.at[i], lhs_sems.at[i]
                    ).start()

                return carry

            lax.fori_loop(0, rows * slots, fetch, 0)
        pool[pool_blocks] = jnp.zeros((block, block), jnp.float32)

        place_rows(tiles_ref, where_ref)

        def list_row(row, carry):
            bases = [base_of(tiles_ref, entry_ref, row, e) * total for e in range(slots)]

            def list_output(o, carry):
                column = column_of(tiles_ref, row, o)
                start = (row * outs + o) * slots
                count = jnp.int32(0)
                for e in range(slots):
                    at = where_ref[bases[e] + column]
                    table_ref[start + count] = at + e * CODE
                    count = count + jnp.where(at != pool_blocks, 1, 0)
                count_ref[row * outs + o] = count
                return carry

            return lax.fori_loop(0, outs, list_output, carry)

        lax.fori_loop(0, rows, list_row, 0)
        for copy in lhs_copies:
            copy.wait()

        def split(index, carry):
            for e in range(4):
                i = index * 4 + e
                if transposed:
                    pltpu.make_async_copy(source_refs[-2].at[0], lhs.at[i], lhs_sems.at[i]).wait()
                value = lhs[i].T if transposed else lhs[i]
                top = value.astype(jnp.bfloat16)
                high[i] = top
                low[i] = (value - top.astype(jnp.float32)).astype(jnp.bfloat16)
            return carry

        lax.fori_loop(0, rows * slots // 4, split, 0)
        for copy in copies:
            copy.wait()

        def term(o, g):
            row = o // outs
            left, right = [], []
            for e in range(GROUP):
                code = table_ref[o * slots + g * GROUP + e]
                s = row * slots + code // CODE
                value = pool[code % CODE]
                top = value.astype(jnp.bfloat16)
                rest = (value - top.astype(jnp.float32)).astype(jnp.bfloat16)
                left.append(jnp.concatenate([high[s], low[s]], axis=0))
                right.append(jnp.concatenate([top, rest], axis=1))
            both = jnp.dot(
                jnp.concatenate(left, axis=1),
                jnp.concatenate(right, axis=0),
                preferred_element_type=jnp.float32,
            )
            upper = both[:block, :block] + both[:block, block:]
            return upper + (both[block:, :block] + both[block:, block:])

        def some_outputs(index, carry):
            first = index * TOGETHER
            steps = count_ref[first]
            for e in range(1, TOGETHER):
                steps = jnp.maximum(steps, count_ref[first + e])
            steps = (steps + GROUP - 1) // GROUP

            def one_group(g, totals):
                return tuple(totals[e] + term(first + e, g) for e in range(TOGETHER))

            zero = jnp.zeros((block, block), jnp.float32)
            totals = lax.fori_loop(0, steps, one_group, (zero,) * TOGETHER)
            for e in range(TOGETHER):
                out_ref[first + e] = totals[e]
            return carry

        lax.fori_loop(0, rows * outs // TOGETHER, some_outputs, 0)

    in_specs = (
        [pl.BlockSpec(memory_space=pltpu.SMEM)]
        + [pl.BlockSpec(memory_space=pl.ANY)] * source_count
    )
    result = pl.pallas_call(
        kernel,
        out_shape=jax.ShapeDtypeStruct((rows * outs, block, block), jnp.float32),
        in_specs=in_specs,
        out_specs=pl.BlockSpec(memory_space=pltpu.VMEM),
        scratch_shapes=[
            pltpu.VMEM((pool_blocks + 1, block, block), jnp.float32),
            pltpu.VMEM((rows * slots, block, block), jnp.float32),
            pltpu.VMEM((rows * slots, block, block), jnp.bfloat16),
            pltpu.VMEM((rows * slots, block, block), jnp.bfloat16),
            pltpu.SemaphoreType.DMA((len(moves),)),
            pltpu.SemaphoreType.DMA((rows * slots,)),
            pltpu.SMEM((rows * outs * slots,), jnp.int32),
            pltpu.SMEM((rows * outs,), jnp.int32),
            pltpu.SMEM((5 * rows * n * rows,), jnp.int32),
            pltpu.SMEM((rows * 2 * slots,), jnp.int32),
        ],
        compiler_params=pltpu.CompilerParams(vmem_limit_bytes=52 * 1024 * 1024),
        cost_estimate=pl.CostEstimate(
            flops=rows * outs * 10 * 6 * block**3 * 4,
            bytes_accessed=(pool_blocks + rows * (slots + outs)) * block * block * 4,
            transcendentals=0,
        ),
    )(tiles, *sources)
    return result.reshape(rows, outs, block, block)


def shards(margin_blocks, margin_cols, factor_blocks, factor_cols, product_cols, metric_cols):
    rows, slots, block = factor_blocks.shape[:3]
    kept, kept_x = product_cols.shape[1], metric_cols.shape[1]
    half_rows, half_kept, half_x = rows // 2, kept // 2, kept_x // 2
    n = lax.axis_size("rows")
    r = lax.axis_index("rows")
    q = lax.axis_index("rep")
    total = n * rows
    mine = margin_blocks.shape[1]
    at_kept, at_margin = slots, slots + kept
    at_metric = at_margin + mine
    at_place = at_metric + kept_x
    ones = jnp.ones((rows, 1), jnp.int32)
    tile = jnp.concatenate(
        [factor_cols, product_cols, margin_cols, metric_cols, r * ones, q * ones], axis=1
    )
    tile = jnp.pad(tile, ((0, 8 - rows), (0, 128 - tile.shape[1])))

    def place_of(tiles):
        return tiles[0, 0, at_place], tiles[0, 0, at_place + 1]

    def place_factor(tiles, where):
        _, mq = place_of(tiles)

        def one_row(near_row, carry):
            slot, inner = near_row // rows, near_row % rows
            swapped = ((inner // half_rows) ^ mq) * half_rows + inner % half_rows
            base = (slot * rows + jnp.where(slot == 0, inner, swapped)) * slots
            for m in range(slots):
                where[near_row * total + tiles[slot, inner, m]] = base + m
            return carry

        lax.fori_loop(0, 5 * rows, one_row, 0)

    def margin_row(tiles, entry, row, k):
        mr, _ = place_of(tiles)
        sign_x = 1 - 2 * (mr % 2)
        sign_y = 2 - 4 * (mr // 2 % 2)
        column = tiles[5 * (k // mine), row, at_margin + k % mine]
        offset = (column // rows - mr + 2 + n) % n - 2
        slot = jnp.where(offset == sign_x, 1, jnp.where(offset == sign_y, 2, 3))
        slot = jnp.where(offset == -sign_x, 4, jnp.where(offset == 0, 0, slot))
        return slot * rows + column % rows

    def product_column(tiles, row, y):
        return tiles[0, row, at_kept + place_of(tiles)[1] * half_kept + y]

    def metric_entries(tiles, where, entry, missing):
        mr, mq = place_of(tiles)

        def each_block(visit):
            def one_row(near_row, carry):
                slot, inner = near_row // rows, near_row % rows
                other = (inner // half_rows) ^ mq
                held = rows + (slot - 1 + 4 * other) * half_rows + inner % half_rows
                base = jnp.where(slot == 0, inner, held) * slots
                for m in range(slots):
                    where[near_row * total + tiles[slot, inner, m]] = visit(base + m)
                return carry

            lax.fori_loop(0, 5 * rows, one_row, 0)

        each_block(lambda at: at + missing + 1)

        def one_column(a, carry):
            count = jnp.int32(0)
            for near_row in range(5 * rows):
                at = where[near_row * total + mr * rows + a]
                entry[a * 2 * slots + count] = (at - missing - 1) * CODE + near_row
                count = count + jnp.where(at != missing, 1, 0)
            return carry

        lax.fori_loop(0, rows, one_column, 0)
        each_block(lambda at: jnp.int32(missing))

    def place_product(tiles, where):
        _, mq = place_of(tiles)

        def one_row(near_row, carry):
            slot, inner = near_row // rows, near_row % rows
            for h in range(2):
                base = ((2 * slot + (h ^ mq)) * rows + inner) * half_kept
                for y in range(half_kept):
                    column = tiles[slot, inner, at_kept + h * half_kept + y]
                    where[near_row * total + column] = base + y
            return carry

        lax.fori_loop(0, 5 * rows, one_row, 0)

    def entry_row(tiles, entry, row, t):
        return entry[row * 2 * slots + t] % CODE

    def metric_column(tiles, row, x):
        return tiles[0, row, at_metric + place_of(tiles)[1] * half_x + x]

    share = half_rows * slots
    flat_factor = factor_blocks.reshape(-1, block, block)
    flat_margin = margin_blocks.reshape(-1, block, block)
    near, tiles = fetch_halo(
        flat_factor, lambda core: core * share, flat_margin, CHUNKS, share // CHUNKS, 0, tile
    )
    moves = [(0, slice(None), 0, rows * slots)]
    for j in range(4):
        for h in range(2):
            moves.append((1, j + 4 * h, ((j + 1) * rows + h * half_rows) * slots, share))
    lhs_moves = []
    for row in range(rows):
        lhs_moves.append((2, pl.ds(row * mine, mine), row * slots, mine))
        lhs_moves.append((1, (8, pl.ds(row * mine, mine)), row * slots + mine, mine))
    product = block_products(
        tiles,
        (place_factor, None, margin_row, product_column),
        [flat_factor, near, flat_margin],
        moves,
        lhs_moves,
        rows,
        slots,
        5 * rows * slots,
        False,
        half_kept,
        n,
    )

    share = rows * half_kept
    flat_product = product.reshape(-1, block, block)
    (near_product,) = fetch_halo(
        flat_product, lambda core: 0, flat_product, CHUNKS, share // CHUNKS, 1
    )
    moves = [(0, slice(None), 0, share), (1, 8, share, share)]
    for j in range(4):
        for h in range(2):
            moves.append((1, j + 4 * h, (2 * j + 2 + h) * share, share))
    metric = block_products(
        tiles,
        (place_product, metric_entries, entry_row, metric_column),
        [flat_product, near_product, flat_factor, near.reshape(-1, block, block)],
        moves,
        [],
        rows,
        slots,
        5 * rows * kept,
        True,
        half_x,
        n,
    )
    return (product, metric)


def solution(mesh):
    return jax.shard_map(
        shards,
        mesh=mesh,
        in_specs=(
            P("rows", "rep", None, None),
            P("rows", "rep"),
            P("rows", None, None, None),
            P("rows", None),
            P("rows", None),
            P("rows", None),
        ),
        out_specs=(P("rows", "rep", None, None), P("rows", "rep", None, None)),
        check_vma=False,
    )
```

```python
import jax
import jax.numpy as jnp
from jax import lax
from jax.experimental import pallas as pl
from jax.experimental.pallas import tpu as pltpu
from jax.sharding import PartitionSpec as P

MESH = pl.DeviceIdType.MESH
CHUNKS = 8
GROUP = 2
TOGETHER = 6
CODE = 1024


def fetch_halo(sent, sent_base, swapped, chunks, size, collective_id, tile=None):
    block = sent.shape[-1]
    at_x, at_y, at_z, at_second, at_swap, at_way = 0, 1, 2, 3, 8, 9

    def kernel(*refs):
        if tile is None:
            sent_ref, swapped_ref, out_ref, send_sem, recv_sem = refs
        else:
            sent_ref, swapped_ref, tile_ref, out_ref, tiles_ref, send_sem, recv_sem, tile_sem = refs
        n = lax.axis_size("rows")
        r = lax.axis_index("rows")
        q = lax.axis_index("rep")
        px, py = r % 2, (r // 2) % 2
        to_x = r + 1 - 2 * px
        to_y = r + 2 - 4 * py
        to_z = (r + n + 4 - 8 * py) % n
        from_z = (r + n - 4 + 8 * py) % n
        outer = px == py
        barrier = pltpu.get_barrier_semaphore()
        for rows, rep in ((to_x, q), (to_y, q), (from_z, q), (r, 1 - q)):
            pl.semaphore_signal(barrier, inc=1, device_id=(rows, rep), device_id_type=MESH)
        pl.semaphore_wait(barrier, 4)

        def span(c):
            return pl.ds(c * size, size)

        def copy(src, kind, place, c, target):
            return pltpu.make_async_remote_copy(
                src_ref=src,
                dst_ref=out_ref.at[place, span(c)],
                send_sem=send_sem.at[kind, c],
                recv_sem=recv_sem.at[place, c],
                device_id=target,
                device_id_type=MESH,
            )

        def own(c):
            return sent_ref.at[pl.ds(sent_base(q) + c * size, size)]

        def over_x(c):
            return copy(own(c), 0, at_x, c, (to_x, q))

        def over_y(c):
            return copy(own(c), 1, at_y, c, (to_y, q))

        def over_z(c):
            return copy(out_ref.at[at_y, span(c)], 2, at_z, c, (to_z, q))

        def second_x(c, held):
            return copy(out_ref.at[held, span(c)], 3, at_second, c, (to_x, q))

        def second_y(c):
            place = jnp.where(outer, at_second, at_way)
            return copy(out_ref.at[at_x, span(c)], 3, place, c, (to_y, q))

        def second_z(c):
            return copy(out_ref.at[at_way, span(c)], 9, at_second, c, (to_z, q))

        def share(place, c):
            return copy(out_ref.at[place, span(c)], 4 + place, 4 + place, c, (r, 1 - q))

        own_share = pltpu.make_async_remote_copy(
            src_ref=swapped_ref,
            dst_ref=out_ref.at[at_swap],
            send_sem=send_sem.at[8, 0],
            recv_sem=recv_sem.at[at_swap, 0],
            device_id=(r, 1 - q),
            device_id_type=MESH,
        )

        def arrived(place, c):
            copy(out_ref.at[place, span(c)], 0, place, c, (r, 1 - q)).wait_recv()

        def tile_copy(src, kind, place, target):
            return pltpu.make_async_remote_copy(
                src_ref=src,
                dst_ref=tiles_ref.at[place],
                send_sem=tile_sem.at[0, kind],
                recv_sem=tile_sem.at[1, place],
                device_id=target,
                device_id_type=MESH,
            )

        tile_hops = []
        if tile is not None:
            tile_hops = [
                tile_copy(tile_ref, 1, 1, (to_x, q)),
                tile_copy(tile_ref, 2, 2, (to_y, q)),
                tile_copy(tile_ref, 5, 5, (r, 1 - q)),
                tile_copy(tiles_ref.at[2], 3, 3, (to_z, q)),
            ]
            own_tile = pltpu.make_async_copy(tile_ref, tiles_ref.at[0], tile_sem.at[0, 0])
            own_tile.start()
            for tile_hop in tile_hops[:3]:
                tile_hop.start()

        pairs = [(c, c + 1) for c in range(0, chunks, 2)]
        x_order = [b for a, b in pairs] + [a for a, b in pairs]
        y_order = [a for a, b in pairs] + [b for a, b in pairs]
        ahead = chunks // 4
        for i in range(ahead):
            over_x(x_order[i]).start()
            over_y(y_order[i]).start()
        if tile is not None:
            tile_hops[1].wait_recv()
            tile_hops[3].start()
        for i in range(chunks):
            c = x_order[i]
            arrived(at_x, c)
            if c % 2:
                second_y(c).start()
            if i + ahead < chunks:
                over_x(x_order[i + ahead]).start()
            share(at_x, c).start()
            if i == 0:
                own_share.start()
            c = y_order[i]
            arrived(at_y, c)
            over_z(c).start()
            if c % 2 == 0:

                @pl.when(outer)
                def _(c=c):
                    second_x(c, at_y).start()

            if i + ahead < chunks:
                over_y(y_order[i + ahead]).start()
            share(at_y, c).start()
            if i >= 1:
                c = y_order[i - 1]
                arrived(at_z, c)
                if c % 2 == 0:

                    @pl.when(jnp.logical_not(outer))
                    def _(c=c):
                        second_x(c, at_z).start()

                share(at_z, c).start()
            if 1 <= i <= len(pairs):
                c = x_order[i - 1]

                @pl.when(outer)
                def _(c=c):
                    arrived(at_way, c)
                    second_z(c).start()

            if i >= len(pairs):
                for c in pairs[i - len(pairs)]:
                    arrived(at_second, c)
                    share(at_second, c).start()
        if tile is not None:
            tile_hops[3].wait_recv()

            @pl.when(outer)
            def _():
                tile_copy(tiles_ref.at[2], 4, 4, (to_x, q)).start()

            @pl.when(jnp.logical_not(outer))
            def _():
                tile_copy(tiles_ref.at[3], 4, 4, (to_x, q)).start()

            tile_hops.append(tile_copy(tiles_ref.at[2], 4, 4, (to_x, q)))
            tile_hops[4].wait_recv()
            tile_hops[0].wait_recv()
            tile_hops[2].wait_recv()
            own_tile.wait()
            for tile_hop in tile_hops:
                tile_hop.wait_send()
        c = y_order[-1]
        arrived(at_z, c)
        share(at_z, c).start()
        for c in range(chunks):
            for place in (4, 5, 6, 7):
                arrived(place, c)
        for c in range(chunks):
            over_x(c).wait_send()
            over_y(c).wait_send()
            over_z(c).wait_send()
            second_x(c, at_z).wait_send()
            if c % 2:

                @pl.when(outer)
                def _(c=c):
                    second_z(c).wait_send()

            for place in (at_x, at_y, at_z, at_second):
                share(place, c).wait_send()
        own_share.wait()

    anywhere = pl.BlockSpec(memory_space=pl.ANY)
    out_shape = [jax.ShapeDtypeStruct((10, chunks * size, block, block), jnp.float32)]
    scratch = [pltpu.SemaphoreType.DMA((10, chunks)), pltpu.SemaphoreType.DMA((10, chunks))]
    operands = [sent, swapped]
    if tile is not None:
        out_shape.append(jax.ShapeDtypeStruct((6,) + tile.shape, tile.dtype))
        scratch.append(pltpu.SemaphoreType.DMA((2, 6)))
        operands.append(tile)
    return pl.pallas_call(
        kernel,
        out_shape=out_shape,
        in_specs=[anywhere] * len(operands),
        out_specs=[anywhere] * len(out_shape),
        scratch_shapes=scratch,
        compiler_params=pltpu.CompilerParams(collective_id=collective_id, has_side_effects=True),
    )(*operands)


def block_products(tiles, build, sources, moves, lhs_moves, rows, slots, pool_blocks, transposed, outs, n):
    block = sources[0].shape[-1]
    source_count = len(sources)

    def kernel(*refs):
        tiles_ref = refs[0]
        source_refs = refs[1 : 1 + source_count]
        out_ref, pool, lhs, high, low, sems, lhs_sems = refs[1 + source_count : 8 + source_count]
        table_ref, count_ref, where_ref, entry_ref = refs[8 + source_count :]

        def moved(index, move, target, semaphores):
            source, at, dst, count = move
            return pltpu.make_async_copy(
                source_refs[source].at[at], target.at[pl.ds(dst, count)], semaphores.at[index]
            )

        lhs_copies = [moved(i, move, lhs, lhs_sems) for i, move in enumerate(lhs_moves)]
        copies = [moved(i, move, pool, sems) for i, move in enumerate(moves)]
        for copy in lhs_copies + copies:
            copy.start()
        total = n * rows

        def clear(i, carry):
            for e in range(slots):
                table_ref[i * slots + e] = jnp.int32(pool_blocks)
            return carry

        lax.fori_loop(0, rows * outs, clear, 0)

        def forget(i, carry):
            for e in range(16):
                where_ref[i * 16 + e] = jnp.int32(pool_blocks)
            return carry

        lax.fori_loop(0, 5 * rows * total // 16, forget, 0)
        place_rows, entries, base_of, column_of = build
        if transposed:
            entries(tiles_ref, where_ref, entry_ref, pool_blocks)
            first, second = source_refs[-2:]
            bound = first.shape[0]

            def fetch(i, carry):
                code = entry_ref[i // slots * 2 * slots + i % slots] // CODE

                @pl.when(code < bound)
                def _():
                    pltpu.make_async_copy(first.at[code], lhs.at[i], lhs_sems.at[i]).start()

                @pl.when(code >= bound)
                def _():
                    pltpu.make_async_copy(
                        second.at[code - bound], lhs.at[i], lhs_sems.at[i]
                    ).start()

                return carry

            lax.fori_loop(0, rows * slots, fetch, 0)
        pool[pool_blocks] = jnp.zeros((block, block), jnp.float32)

        place_rows(tiles_ref, where_ref)

        def list_row(row, carry):
            bases = [base_of(tiles_ref, entry_ref, row, e) * total for e in range(slots)]

            def list_output(o, carry):
                column = column_of(tiles_ref, row, o)
                start = (row * outs + o) * slots
                count = jnp.int32(0)
                for e in range(slots):
                    at = where_ref[bases[e] + column]
                    table_ref[start + count] = at + e * CODE
                    count = count + jnp.where(at != pool_blocks, 1, 0)
                count_ref[row * outs + o] = count
                return carry

            return lax.fori_loop(0, outs, list_output, carry)

        lax.fori_loop(0, rows, list_row, 0)
        for copy in lhs_copies:
            copy.wait()

        def split(index, carry):
            for e in range(4):
                i = index * 4 + e
                if transposed:
                    pltpu.make_async_copy(source_refs[-2].at[0], lhs.at[i], lhs_sems.at[i]).wait()
                value = lhs[i].T if transposed else lhs[i]
                top = value.astype(jnp.bfloat16)
                high[i] = top
                low[i] = (value - top.astype(jnp.float32)).astype(jnp.bfloat16)
            return carry

        lax.fori_loop(0, rows * slots // 4, split, 0)
        for copy in copies:
            copy.wait()

        def term(o, g):
            row = o // outs
            left, right = [], []
            for e in range(GROUP):
                code = table_ref[o * slots + g * GROUP + e]
                s = row * slots + code // CODE
                value = pool[code % CODE]
                top = value.astype(jnp.bfloat16)
                rest = (value - top.astype(jnp.float32)).astype(jnp.bfloat16)
                left.append(jnp.concatenate([high[s], low[s]], axis=0))
                right.append(jnp.concatenate([top, rest], axis=1))
            both = jnp.dot(
                jnp.concatenate(left, axis=1),
                jnp.concatenate(right, axis=0),
                preferred_element_type=jnp.float32,
            )
            upper = both[:block, :block] + both[:block, block:]
            return upper + (both[block:, :block] + both[block:, block:])

        def some_outputs(index, carry):
            first = index * TOGETHER
            steps = count_ref[first]
            for e in range(1, TOGETHER):
                steps = jnp.maximum(steps, count_ref[first + e])
            steps = (steps + GROUP - 1) // GROUP

            def one_group(g, totals):
                return tuple(totals[e] + term(first + e, g) for e in range(TOGETHER))

            zero = jnp.zeros((block, block), jnp.float32)
            totals = lax.fori_loop(0, steps, one_group, (zero,) * TOGETHER)
            for e in range(TOGETHER):
                out_ref[first + e] = totals[e]
            return carry

        lax.fori_loop(0, rows * outs // TOGETHER, some_outputs, 0)

    in_specs = (
        [pl.BlockSpec(memory_space=pltpu.SMEM)]
        + [pl.BlockSpec(memory_space=pl.ANY)] * source_count
    )
    result = pl.pallas_call(
        kernel,
        out_shape=jax.ShapeDtypeStruct((rows * outs, block, block), jnp.float32),
        in_specs=in_specs,
        out_specs=pl.BlockSpec(memory_space=pltpu.VMEM),
        scratch_shapes=[
            pltpu.VMEM((pool_blocks + 1, block, block), jnp.float32),
            pltpu.VMEM((rows * slots, block, block), jnp.float32),
            pltpu.VMEM((rows * slots, block, block), jnp.bfloat16),
            pltpu.VMEM((rows * slots, block, block), jnp.bfloat16),
            pltpu.SemaphoreType.DMA((len(moves),)),
            pltpu.SemaphoreType.DMA((rows * slots,)),
            pltpu.SMEM((rows * outs * slots,), jnp.int32),
            pltpu.SMEM((rows * outs,), jnp.int32),
            pltpu.SMEM((5 * rows * n * rows,), jnp.int32),
            pltpu.SMEM((rows * 2 * slots,), jnp.int32),
        ],
        compiler_params=pltpu.CompilerParams(vmem_limit_bytes=52 * 1024 * 1024),
        cost_estimate=pl.CostEstimate(
            flops=rows * outs * 10 * 6 * block**3 * 4,
            bytes_accessed=(pool_blocks + rows * (slots + outs)) * block * block * 4,
            transcendentals=0,
        ),
    )(tiles, *sources)
    return result.reshape(rows, outs, block, block)


def shards(margin_blocks, margin_cols, factor_blocks, factor_cols, product_cols, metric_cols):
    rows, slots, block = factor_blocks.shape[:3]
    kept, kept_x = product_cols.shape[1], metric_cols.shape[1]
    half_rows, half_kept, half_x = rows // 2, kept // 2, kept_x // 2
    n = lax.axis_size("rows")
    r = lax.axis_index("rows")
    q = lax.axis_index("rep")
    total = n * rows
    mine = margin_blocks.shape[1]
    at_kept, at_margin = slots, slots + kept
    at_metric = at_margin + mine
    at_place = at_metric + kept_x
    ones = jnp.ones((rows, 1), jnp.int32)
    tile = jnp.concatenate(
        [factor_cols, product_cols, margin_cols, metric_cols, r * ones, q * ones], axis=1
    )
    tile = jnp.pad(tile, ((0, 8 - rows), (0, 128 - tile.shape[1])))

    def place_of(tiles):
        return tiles[0, 0, at_place], tiles[0, 0, at_place + 1]

    def place_factor(tiles, where):
        _, mq = place_of(tiles)

        def one_row(near_row, carry):
            slot, inner = near_row // rows, near_row % rows
            swapped = ((inner // half_rows) ^ mq) * half_rows + inner % half_rows
            base = (slot * rows + jnp.where(slot == 0, inner, swapped)) * slots
            for m in range(slots):
                where[near_row * total + tiles[slot, inner, m]] = base + m
            return carry

        lax.fori_loop(0, 5 * rows, one_row, 0)

    def margin_row(tiles, entry, row, k):
        mr, _ = place_of(tiles)
        sign_x = 1 - 2 * (mr % 2)
        sign_y = 2 - 4 * (mr // 2 % 2)
        column = tiles[5 * (k // mine), row, at_margin + k % mine]
        offset = (column // rows - mr + 2 + n) % n - 2
        slot = jnp.where(offset == sign_x, 1, jnp.where(offset == sign_y, 2, 3))
        slot = jnp.where(offset == -sign_x, 4, jnp.where(offset == 0, 0, slot))
        return slot * rows + column % rows

    def product_column(tiles, row, y):
        return tiles[0, row, at_kept + place_of(tiles)[1] * half_kept + y]

    def metric_entries(tiles, where, entry, missing):
        mr, mq = place_of(tiles)

        def each_block(visit):
            def one_row(near_row, carry):
                slot, inner = near_row // rows, near_row % rows
                other = (inner // half_rows) ^ mq
                held = rows + (slot - 1 + 4 * other) * half_rows + inner % half_rows
                base = jnp.where(slot == 0, inner, held) * slots
                for m in range(slots):
                    where[near_row * total + tiles[slot, inner, m]] = visit(base + m)
                return carry

            lax.fori_loop(0, 5 * rows, one_row, 0)

        each_block(lambda at: at + missing + 1)

        def one_column(a, carry):
            count = jnp.int32(0)
            for near_row in range(5 * rows):
                at = where[near_row * total + mr * rows + a]
                entry[a * 2 * slots + count] = (at - missing - 1) * CODE + near_row
                count = count + jnp.where(at != missing, 1, 0)
            return carry

        lax.fori_loop(0, rows, one_column, 0)
        each_block(lambda at: jnp.int32(missing))

    def place_product(tiles, where):
        _, mq = place_of(tiles)

        def one_row(near_row, carry):
            slot, inner = near_row // rows, near_row % rows
            for h in range(2):
                base = ((2 * slot + (h ^ mq)) * rows + inner) * half_kept
                for y in range(half_kept):
                    column = tiles[slot, inner, at_kept + h * half_kept + y]
                    where[near_row * total + column] = base + y
            return carry

        lax.fori_loop(0, 5 * rows, one_row, 0)

    def entry_row(tiles, entry, row, t):
        return entry[row * 2 * slots + t] % CODE

    def metric_column(tiles, row, x):
        return tiles[0, row, at_metric + place_of(tiles)[1] * half_x + x]

    share = half_rows * slots
    flat_factor = factor_blocks.reshape(-1, block, block)
    flat_margin = margin_blocks.reshape(-1, block, block)
    near, tiles = fetch_halo(
        flat_factor, lambda core: core * share, flat_margin, CHUNKS, share // CHUNKS, 0, tile
    )
    moves = [(0, slice(None), 0, rows * slots)]
    for j in range(4):
        for h in range(2):
            moves.append((1, j + 4 * h, ((j + 1) * rows + h * half_rows) * slots, share))
    lhs_moves = []
    for row in range(rows):
        lhs_moves.append((2, pl.ds(row * mine, mine), row * slots, mine))
        lhs_moves.append((1, (8, pl.ds(row * mine, mine)), row * slots + mine, mine))
    product = block_products(
        tiles,
        (place_factor, None, margin_row, product_column),
        [flat_factor, near, flat_margin],
        moves,
        lhs_moves,
        rows,
        slots,
        5 * rows * slots,
        False,
        half_kept,
        n,
    )

    share = rows * half_kept
    flat_product = product.reshape(-1, block, block)
    (near_product,) = fetch_halo(
        flat_product, lambda core: 0, flat_product, CHUNKS, share // CHUNKS, 1
    )
    moves = [(0, slice(None), 0, share), (1, 8, share, share)]
    for j in range(4):
        for h in range(2):
            moves.append((1, j + 4 * h, (2 * j + 2 + h) * share, share))
    metric = block_products(
        tiles,
        (place_product, metric_entries, entry_row, metric_column),
        [flat_product, near_product, flat_factor, near.reshape(-1, block, block)],
        moves,
        [],
        rows,
        slots,
        5 * rows * kept,
        True,
        half_x,
        n,
    )
    return (product, metric)


def solution(mesh):
    return jax.shard_map(
        shards,
        mesh=mesh,
        in_specs=(
            P("rows", "rep", None, None),
            P("rows", "rep"),
            P("rows", None, None, None),
            P("rows", None),
            P("rows", None),
            P("rows", None),
        ),
        out_specs=(P("rows", "rep", None, None), P("rows", "rep", None, None)),
        check_vma=False,
    )
```

```python
import jax
import jax.numpy as jnp
from jax import lax
from jax.experimental import pallas as pl
from jax.experimental.pallas import tpu as pltpu
from jax.sharding import PartitionSpec as P

MESH = pl.DeviceIdType.MESH
CHUNKS = 8
GROUP = 4
TOGETHER = 4
CODE = 1024


def fetch_halo(sent, sent_base, swapped, chunks, size, collective_id, tile=None):
    block = sent.shape[-1]
    at_x, at_y, at_z, at_second, at_swap, at_way = 0, 1, 2, 3, 8, 9

    def kernel(*refs):
        if tile is None:
            sent_ref, swapped_ref, out_ref, send_sem, recv_sem = refs
        else:
            sent_ref, swapped_ref, tile_ref, out_ref, tiles_ref, send_sem, recv_sem, tile_sem = refs
        n = lax.axis_size("rows")
        r = lax.axis_index("rows")
        q = lax.axis_index("rep")
        px, py = r % 2, (r // 2) % 2
        to_x = r + 1 - 2 * px
        to_y = r + 2 - 4 * py
        to_z = (r + n + 4 - 8 * py) % n
        from_z = (r + n - 4 + 8 * py) % n
        outer = px == py
        barrier = pltpu.get_barrier_semaphore()
        for rows, rep in ((to_x, q), (to_y, q), (from_z, q), (r, 1 - q)):
            pl.semaphore_signal(barrier, inc=1, device_id=(rows, rep), device_id_type=MESH)
        pl.semaphore_wait(barrier, 4)

        def span(c):
            return pl.ds(c * size, size)

        def copy(src, kind, place, c, target):
            return pltpu.make_async_remote_copy(
                src_ref=src,
                dst_ref=out_ref.at[place, span(c)],
                send_sem=send_sem.at[kind, c],
                recv_sem=recv_sem.at[place, c],
                device_id=target,
                device_id_type=MESH,
            )

        def own(c):
            return sent_ref.at[pl.ds(sent_base(q) + c * size, size)]

        def over_x(c):
            return copy(own(c), 0, at_x, c, (to_x, q))

        def over_y(c):
            return copy(own(c), 1, at_y, c, (to_y, q))

        def over_z(c):
            return copy(out_ref.at[at_y, span(c)], 2, at_z, c, (to_z, q))

        def second_x(c, held):
            return copy(out_ref.at[held, span(c)], 3, at_second, c, (to_x, q))

        def second_y(c):
            place = jnp.where(outer, at_second, at_way)
            return copy(out_ref.at[at_x, span(c)], 3, place, c, (to_y, q))

        def second_z(c):
            return copy(out_ref.at[at_way, span(c)], 9, at_second, c, (to_z, q))

        def share(place, c):
            return copy(out_ref.at[place, span(c)], 4 + place, 4 + place, c, (r, 1 - q))

        own_share = pltpu.make_async_remote_copy(
            src_ref=swapped_ref,
            dst_ref=out_ref.at[at_swap],
            send_sem=send_sem.at[8, 0],
            recv_sem=recv_sem.at[at_swap, 0],
            device_id=(r, 1 - q),
            device_id_type=MESH,
        )

        def arrived(place, c):
            copy(out_ref.at[place, span(c)], 0, place, c, (r, 1 - q)).wait_recv()

        def tile_copy(src, kind, place, target):
            return pltpu.make_async_remote_copy(
                src_ref=src,
                dst_ref=tiles_ref.at[place],
                send_sem=tile_sem.at[0, kind],
                recv_sem=tile_sem.at[1, place],
                device_id=target,
                device_id_type=MESH,
            )

        tile_hops = []
        if tile is not None:
            tile_hops = [
                tile_copy(tile_ref, 1, 1, (to_x, q)),
                tile_copy(tile_ref, 2, 2, (to_y, q)),
                tile_copy(tile_ref, 5, 5, (r, 1 - q)),
                tile_copy(tiles_ref.at[2], 3, 3, (to_z, q)),
            ]
            own_tile = pltpu.make_async_copy(tile_ref, tiles_ref.at[0], tile_sem.at[0, 0])
            own_tile.start()
            for tile_hop in tile_hops[:3]:
                tile_hop.start()

        pairs = [(c, c + 1) for c in range(0, chunks, 2)]
        x_order = [b for a, b in pairs] + [a for a, b in pairs]
        y_order = [a for a, b in pairs] + [b for a, b in pairs]
        ahead = chunks // 4
        for i in range(ahead):
            over_x(x_order[i]).start()
            over_y(y_order[i]).start()
        if tile is not None:
            tile_hops[1].wait_recv()
            tile_hops[3].start()
        for i in range(chunks):
            c = x_order[i]
            arrived(at_x, c)
            if c % 2:
                second_y(c).start()
            if i + ahead < chunks:
                over_x(x_order[i + ahead]).start()
            share(at_x, c).start()
            if i == 0:
                own_share.start()
            c = y_order[i]
            arrived(at_y, c)
            over_z(c).start()
            if c % 2 == 0:

                @pl.when(outer)
                def _(c=c):
                    second_x(c, at_y).start()

            if i + ahead < chunks:
                over_y(y_order[i + ahead]).start()
            share(at_y, c).start()
            if i >= 1:
                c = y_order[i - 1]
                arrived(at_z, c)
                if c % 2 == 0:

                    @pl.when(jnp.logical_not(outer))
                    def _(c=c):
                        second_x(c, at_z).start()

                share(at_z, c).start()
            if 1 <= i <= len(pairs):
                c = x_order[i - 1]

                @pl.when(outer)
                def _(c=c):
                    arrived(at_way, c)
                    second_z(c).start()

            if i >= len(pairs):
                for c in pairs[i - len(pairs)]:
                    arrived(at_second, c)
                    share(at_second, c).start()
        if tile is not None:
            tile_hops[3].wait_recv()

            @pl.when(outer)
            def _():
                tile_copy(tiles_ref.at[2], 4, 4, (to_x, q)).start()

            @pl.when(jnp.logical_not(outer))
            def _():
                tile_copy(tiles_ref.at[3], 4, 4, (to_x, q)).start()

            tile_hops.append(tile_copy(tiles_ref.at[2], 4, 4, (to_x, q)))
            tile_hops[4].wait_recv()
            tile_hops[0].wait_recv()
            tile_hops[2].wait_recv()
            own_tile.wait()
            for tile_hop in tile_hops:
                tile_hop.wait_send()
        c = y_order[-1]
        arrived(at_z, c)
        share(at_z, c).start()
        for c in range(chunks):
            for place in (4, 5, 6, 7):
                arrived(place, c)
        for c in range(chunks):
            over_x(c).wait_send()
            over_y(c).wait_send()
            over_z(c).wait_send()
            second_x(c, at_z).wait_send()
            if c % 2:

                @pl.when(outer)
                def _(c=c):
                    second_z(c).wait_send()

            for place in (at_x, at_y, at_z, at_second):
                share(place, c).wait_send()
        own_share.wait()

    anywhere = pl.BlockSpec(memory_space=pl.ANY)
    out_shape = [jax.ShapeDtypeStruct((10, chunks * size, block, block), jnp.float32)]
    scratch = [pltpu.SemaphoreType.DMA((10, chunks)), pltpu.SemaphoreType.DMA((10, chunks))]
    operands = [sent, swapped]
    if tile is not None:
        out_shape.append(jax.ShapeDtypeStruct((6,) + tile.shape, tile.dtype))
        scratch.append(pltpu.SemaphoreType.DMA((2, 6)))
        operands.append(tile)
    return pl.pallas_call(
        kernel,
        out_shape=out_shape,
        in_specs=[anywhere] * len(operands),
        out_specs=[anywhere] * len(out_shape),
        scratch_shapes=scratch,
        compiler_params=pltpu.CompilerParams(collective_id=collective_id, has_side_effects=True),
    )(*operands)


def block_products(tiles, build, sources, moves, lhs_moves, rows, slots, pool_blocks, transposed, outs, n):
    block = sources[0].shape[-1]
    source_count = len(sources)

    def kernel(*refs):
        tiles_ref = refs[0]
        source_refs = refs[1 : 1 + source_count]
        out_ref, pool, lhs, high, low, sems, lhs_sems = refs[1 + source_count : 8 + source_count]
        table_ref, count_ref, where_ref, entry_ref = refs[8 + source_count :]

        def moved(index, move, target, semaphores):
            source, at, dst, count = move
            return pltpu.make_async_copy(
                source_refs[source].at[at], target.at[pl.ds(dst, count)], semaphores.at[index]
            )

        lhs_copies = [moved(i, move, lhs, lhs_sems) for i, move in enumerate(lhs_moves)]
        copies = [moved(i, move, pool, sems) for i, move in enumerate(moves)]
        early = len(copies) // 3 if transposed else len(copies)
        for copy in lhs_copies + copies[:early]:
            copy.start()
        total = n * rows

        def clear(i, carry):
            for e in range(slots):
                table_ref[i * slots + e] = jnp.int32(pool_blocks)
            return carry

        lax.fori_loop(0, rows * outs, clear, 0)

        def forget(i, carry):
            for e in range(16):
                where_ref[i * 16 + e] = jnp.int32(pool_blocks)
            return carry

        lax.fori_loop(0, 5 * rows * total // 16, forget, 0)
        place_rows, entries, base_of, column_of = build
        if transposed:
            entries(tiles_ref, where_ref, entry_ref, pool_blocks)
            first, second = source_refs[-2:]
            bound = first.shape[0]

            def fetch(i, carry):
                code = entry_ref[i // slots * 2 * slots + i % slots] // CODE

                @pl.when(code < bound)
                def _():
                    pltpu.make_async_copy(first.at[code], lhs.at[i], lhs_sems.at[i]).start()

                @pl.when(code >= bound)
                def _():
                    pltpu.make_async_copy(
                        second.at[code - bound], lhs.at[i], lhs_sems.at[i]
                    ).start()

                return carry

            lax.fori_loop(0, rows * slots, fetch, 0)
        for copy in copies[early:]:
            copy.start()
        pool[pool_blocks] = jnp.zeros((block, block), jnp.float32)

        place_rows(tiles_ref, where_ref)

        def list_row(row, carry):
            bases = [base_of(tiles_ref, entry_ref, row, e) * total for e in range(slots)]

            def list_output(o, carry):
                column = column_of(tiles_ref, row, o)
                start = (row * outs + o) * slots
                count = jnp.int32(0)
                for e in range(slots):
                    at = where_ref[bases[e] + column]
                    table_ref[start + count] = at + e * CODE
                    count = count + jnp.where(at != pool_blocks, 1, 0)
                count_ref[row * outs + o] = count
                return carry

            return lax.fori_loop(0, outs, list_output, carry)

        lax.fori_loop(0, rows, list_row, 0)
        for copy in lhs_copies:
            copy.wait()

        def split(index, carry):
            for e in range(4):
                i = index * 4 + e
                if transposed:
                    pltpu.make_async_copy(source_refs[-2].at[0], lhs.at[i], lhs_sems.at[i]).wait()
                value = lhs[i].T if transposed else lhs[i]
                top = value.astype(jnp.bfloat16)
                high[i] = top
                low[i] = (value - top.astype(jnp.float32)).astype(jnp.bfloat16)
            return carry

        lax.fori_loop(0, rows * slots // 4, split, 0)
        for copy in copies:
            copy.wait()

        def term(o, g):
            row = o // outs
            left, right = [], []
            for e in range(GROUP):
                code = table_ref[o * slots + g * GROUP + e]
                s = row * slots + code // CODE
                value = pool[code % CODE]
                top = value.astype(jnp.bfloat16)
                rest = (value - top.astype(jnp.float32)).astype(jnp.bfloat16)
                left.append(jnp.concatenate([high[s], low[s]], axis=0))
                right.append(jnp.concatenate([top, rest], axis=1))
            both = jnp.dot(
                jnp.concatenate(left, axis=1),
                jnp.concatenate(right, axis=0),
                preferred_element_type=jnp.float32,
            )
            upper = both[:block, :block] + both[:block, block:]
            return upper + (both[block:, :block] + both[block:, block:])

        def some_outputs(index, carry):
            first = index * TOGETHER
            steps = count_ref[first]
            for e in range(1, TOGETHER):
                steps = jnp.maximum(steps, count_ref[first + e])
            steps = (steps + GROUP - 1) // GROUP

            def one_group(g, totals):
                return tuple(totals[e] + term(first + e, g) for e in range(TOGETHER))

            zero = jnp.zeros((block, block), jnp.float32)
            totals = lax.fori_loop(0, steps, one_group, (zero,) * TOGETHER)
            for e in range(TOGETHER):
                out_ref[first + e] = totals[e]
            return carry

        lax.fori_loop(0, rows * outs // TOGETHER, some_outputs, 0)

    in_specs = (
        [pl.BlockSpec(memory_space=pltpu.SMEM)]
        + [pl.BlockSpec(memory_space=pl.ANY)] * source_count
    )
    result = pl.pallas_call(
        kernel,
        out_shape=jax.ShapeDtypeStruct((rows * outs, block, block), jnp.float32),
        in_specs=in_specs,
        out_specs=pl.BlockSpec(memory_space=pltpu.VMEM),
        scratch_shapes=[
            pltpu.VMEM((pool_blocks + 1, block, block), jnp.float32),
            pltpu.VMEM((rows * slots, block, block), jnp.float32),
            pltpu.VMEM((rows * slots, block, block), jnp.bfloat16),
            pltpu.VMEM((rows * slots, block, block), jnp.bfloat16),
            pltpu.SemaphoreType.DMA((len(moves),)),
            pltpu.SemaphoreType.DMA((rows * slots,)),
            pltpu.SMEM((rows * outs * slots,), jnp.int32),
            pltpu.SMEM((rows * outs,), jnp.int32),
            pltpu.SMEM((5 * rows * n * rows,), jnp.int32),
            pltpu.SMEM((rows * 2 * slots,), jnp.int32),
        ],
        compiler_params=pltpu.CompilerParams(vmem_limit_bytes=52 * 1024 * 1024),
        cost_estimate=pl.CostEstimate(
            flops=rows * outs * 10 * 6 * block**3 * 4,
            bytes_accessed=(pool_blocks + rows * (slots + outs)) * block * block * 4,
            transcendentals=0,
        ),
    )(tiles, *sources)
    return result.reshape(rows, outs, block, block)


def shards(margin_blocks, margin_cols, factor_blocks, factor_cols, product_cols, metric_cols):
    rows, slots, block = factor_blocks.shape[:3]
    kept, kept_x = product_cols.shape[1], metric_cols.shape[1]
    half_rows, half_kept, half_x = rows // 2, kept // 2, kept_x // 2
    n = lax.axis_size("rows")
    r = lax.axis_index("rows")
    q = lax.axis_index("rep")
    total = n * rows
    mine = margin_blocks.shape[1]
    at_kept, at_margin = slots, slots + kept
    at_metric = at_margin + mine
    at_place = at_metric + kept_x
    ones = jnp.ones((rows, 1), jnp.int32)
    tile = jnp.concatenate(
        [factor_cols, product_cols, margin_cols, metric_cols, r * ones, q * ones], axis=1
    )
    tile = jnp.pad(tile, ((0, 8 - rows), (0, 128 - tile.shape[1])))

    def place_of(tiles):
        return tiles[0, 0, at_place], tiles[0, 0, at_place + 1]

    def place_factor(tiles, where):
        _, mq = place_of(tiles)

        def one_row(near_row, carry):
            slot, inner = near_row // rows, near_row % rows
            swapped = ((inner // half_rows) ^ mq) * half_rows + inner % half_rows
            base = (slot * rows + jnp.where(slot == 0, inner, swapped)) * slots
            for m in range(slots):
                where[near_row * total + tiles[slot, inner, m]] = base + m
            return carry

        lax.fori_loop(0, 5 * rows, one_row, 0)

    def margin_row(tiles, entry, row, k):
        mr, _ = place_of(tiles)
        sign_x = 1 - 2 * (mr % 2)
        sign_y = 2 - 4 * (mr // 2 % 2)
        column = tiles[5 * (k // mine), row, at_margin + k % mine]
        offset = (column // rows - mr + 2 + n) % n - 2
        slot = jnp.where(offset == sign_x, 1, jnp.where(offset == sign_y, 2, 3))
        slot = jnp.where(offset == -sign_x, 4, jnp.where(offset == 0, 0, slot))
        return slot * rows + column % rows

    def product_column(tiles, row, y):
        return tiles[0, row, at_kept + place_of(tiles)[1] * half_kept + y]

    def metric_entries(tiles, where, entry, missing):
        mr, mq = place_of(tiles)

        def each_block(visit):
            def one_row(near_row, carry):
                slot, inner = near_row // rows, near_row % rows
                other = (inner // half_rows) ^ mq
                held = rows + (slot - 1 + 4 * other) * half_rows + inner % half_rows
                base = jnp.where(slot == 0, inner, held) * slots
                for m in range(slots):
                    where[near_row * total + tiles[slot, inner, m]] = visit(base + m)
                return carry

            lax.fori_loop(0, 5 * rows, one_row, 0)

        each_block(lambda at: at + missing + 1)

        def one_column(a, carry):
            count = jnp.int32(0)
            for near_row in range(5 * rows):
                at = where[near_row * total + mr * rows + a]
                entry[a * 2 * slots + count] = (at - missing - 1) * CODE + near_row
                count = count + jnp.where(at != missing, 1, 0)
            return carry

        lax.fori_loop(0, rows, one_column, 0)
        each_block(lambda at: jnp.int32(missing))

    def place_product(tiles, where):
        _, mq = place_of(tiles)

        def one_row(near_row, carry):
            slot, inner = near_row // rows, near_row % rows
            for h in range(2):
                base = ((2 * slot + (h ^ mq)) * rows + inner) * half_kept
                for y in range(half_kept):
                    column = tiles[slot, inner, at_kept + h * half_kept + y]
                    where[near_row * total + column] = base + y
            return carry

        lax.fori_loop(0, 5 * rows, one_row, 0)

    def entry_row(tiles, entry, row, t):
        return entry[row * 2 * slots + t] % CODE

    def metric_column(tiles, row, x):
        return tiles[0, row, at_metric + place_of(tiles)[1] * half_x + x]

    share = half_rows * slots
    flat_factor = factor_blocks.reshape(-1, block, block)
    flat_margin = margin_blocks.reshape(-1, block, block)
    near, tiles = fetch_halo(
        flat_factor, lambda core: core * share, flat_margin, CHUNKS, share // CHUNKS, 0, tile
    )
    moves = [(0, slice(None), 0, rows * slots)]
    for j in range(4):
        for h in range(2):
            moves.append((1, j + 4 * h, ((j + 1) * rows + h * half_rows) * slots, share))
    lhs_moves = []
    for row in range(rows):
        lhs_moves.append((2, pl.ds(row * mine, mine), row * slots, mine))
        lhs_moves.append((1, (8, pl.ds(row * mine, mine)), row * slots + mine, mine))
    product = block_products(
        tiles,
        (place_factor, None, margin_row, product_column),
        [flat_factor, near, flat_margin],
        moves,
        lhs_moves,
        rows,
        slots,
        5 * rows * slots,
        False,
        half_kept,
        n,
    )

    share = rows * half_kept
    flat_product = product.reshape(-1, block, block)
    (near_product,) = fetch_halo(
        flat_product, lambda core: 0, flat_product, CHUNKS, share // CHUNKS, 1
    )
    moves = [(0, slice(None), 0, share), (1, 8, share, share)]
    for j in range(4):
        for h in range(2):
            moves.append((1, j + 4 * h, (2 * j + 2 + h) * share, share))
    metric = block_products(
        tiles,
        (place_product, metric_entries, entry_row, metric_column),
        [flat_product, near_product, flat_factor, near.reshape(-1, block, block)],
        moves,
        [],
        rows,
        slots,
        5 * rows * kept,
        True,
        half_x,
        n,
    )
    return (product, metric)


def solution(mesh):
    return jax.shard_map(
        shards,
        mesh=mesh,
        in_specs=(
            P("rows", "rep", None, None),
            P("rows", "rep"),
            P("rows", None, None, None),
            P("rows", None),
            P("rows", None),
            P("rows", None),
        ),
        out_specs=(P("rows", "rep", None, None), P("rows", "rep", None, None)),
        check_vma=False,
    )
```
